32 devices in a mesh: ctx: 16 (over z, y, core), tp: 2 (over x).
Axes of the slice: x: 2, y: 2, z: 4, core: 2. Of those that a mesh axis runs over, the one named last changes fastest.
Arguments:
- hidden_in: bfloat16 [2048, 1536], P('ctx', 'tp'), may hold values from -60 to 60
- queries: bfloat16 [2048, 2048], P('ctx', 'tp'), may hold values from -200 to 200
- rotated_key_value: bfloat16 [2048, 4, 128], P('ctx', 'tp'), may hold values from -5 to 5
- sink_logit_table: float32 [32], P('tp'), may hold values from -2 to 2
- out_proj: bfloat16 [2048, 1536], P('tp', 'ctx'), may hold values from -0.125 to 0.125
- norm_gain: float32 [1536], P('tp'), may hold values from 0.1 to 1.9
- expert_in: bfloat16 [16, 2, 1536, 1536], P('ctx', None, None, 'tp'), may hold values from -0.15625 to 0.15625
- expert_out: bfloat16 [16, 1536, 1536], P('ctx', 'tp'), may hold values from -0.15625 to 0.15625
- routes: int32 [2048, 4], P('ctx'), may hold values from 0 to 15, all different within a row; in each aligned block of 128 rows (0 to 127, 128 to 255, ...) at most 96 rows name the same one
- route_scores: float32 [2048, 4], P('ctx'), may hold values from 0.05 to 1
Outputs:
- layer_out: bfloat16 [2048, 1536], P('ctx', 'tp')
The draws below stay inside these ranges and needn't reach their ends.
Inputs may be any that keep to these rules, and one draw needn't show every extreme that they name: `routes`: each token names 4 different experts. In every aligned block of 128 tokens (the tokens of one device) no expert is named by more than 96 tokens, a bound that some block reaches.
All inputs are finite; a program needn't handle non-finite values.
Results may differ from the reference program's by a relative error of at most 0.008.
Values may be sent and summed in bfloat16 or wider, within the bound.
A program may use at most 64 MiB of HBM per device.

```python
import math
import jax
import jax.numpy as jnp
import numpy as np
from jax import lax

D = 1536
FF = 1536
QUERY_HEADS = 32
KEY_VALUE_HEADS = 4
HEAD_SIZE = 64
TOP = 4
WINDOW_KEYS = 128
TOK_DEV = 128
EXPERTS = 16
TOKEN_TOTAL = 2048
CAP = 96
N_CTX = 16
N_TP = 2


def attention_base(key):
    query_key = jax.random.fold_in(key, 101)
    paired_key = jax.random.fold_in(key, 102)
    query_matrix = jnp.clip(jax.random.normal(query_key, (TOKEN_TOTAL, QUERY_HEADS, HEAD_SIZE), jnp.float32), -5.0, 5.0)
    paired_value = jnp.clip(jax.random.normal(paired_key, (TOKEN_TOTAL, KEY_VALUE_HEADS, 2, HEAD_SIZE), jnp.float32), -5.0, 5.0)
    return (query_matrix.reshape(TOKEN_TOTAL, QUERY_HEADS * HEAD_SIZE), paired_value.reshape(TOKEN_TOTAL, KEY_VALUE_HEADS, 2 * HEAD_SIZE))


def draw_queries(key, part):
    return attention_base(key)[0].astype(jnp.bfloat16)


def draw_rotated_key_value(key, part):
    return attention_base(key)[1].astype(jnp.bfloat16)


def draw_hidden_in(key, part):
    noise_key = jax.random.fold_in(key, 201)
    column_key = jax.random.fold_in(key, 202)
    row_key = jax.random.fold_in(key, 203)
    noise = jnp.clip(jax.random.normal(noise_key, (TOKEN_TOTAL, D), jnp.float32), -5.0, 5.0)
    ramp = 3.0 ** (jnp.arange(D, dtype=jnp.float32) / D - 0.5)
    columns = jnp.exp(jax.random.uniform(column_key, (D,), jnp.float32, math.log(0.3), math.log(3.0))) * ramp
    row_scale = jnp.exp(jax.random.uniform(row_key, (TOKEN_TOTAL, 1), jnp.float32, math.log(0.5), math.log(2.0)))
    values = noise * columns * row_scale
    return values.astype(jnp.bfloat16)


def block_scale(own_key, dims, split, least, top_value):
    level, own = 1.0, jax.random.fold_in(own_key, 6)
    for axis_at, shards_of in split:
        steps = jnp.exp(jax.random.uniform(jax.random.fold_in(own, axis_at), (shards_of,), jnp.float32, least / len(split), top_value / len(split)))
        level = level * jnp.repeat(steps, dims[axis_at] // shards_of).reshape([-1 if axis == axis_at else 1 for axis in range(len(dims))])
    return level


def shared_out(own_key, own, number, rows, count, top, reach, lean):
    order = jax.random.permutation(own_key, count)
    packed, ordinary = portions_of(count, rows * top, reach, lean, True), portions_of(count, rows * top, reach, lean, False)
    places = jnp.arange(count)

    def named(lengths, rotation):
        used = int((lengths > 0).sum())
        fixed = max(1, used // 4)
        moved = fixed + (places - fixed + rotation * (used - fixed)) % max(1, count - fixed)
        return jnp.zeros((count,), jnp.int32).at[order[jnp.where(places < fixed, places, moved)]].set(jnp.asarray(lengths, jnp.int32))

    lengths = jnp.where(number % 4 == 0, named(packed, number // 4), named(ordinary, number - number // 4 - 1))
    mixed = jax.random.permutation(jax.random.fold_in(own, 3), count)
    giver, taker = mixed[0:count // 2 * 2:2], mixed[1:count // 2 * 2:2]
    margin = jnp.minimum(lengths[giver] - 1, reach - lengths[taker]) // 2
    margin = jnp.where((giver == order[0]) | (taker == order[0]) | (lengths[taker] == 0), 0, jnp.maximum(margin, 0))
    moved = jax.random.randint(jax.random.fold_in(own, 4), (count // 2,), 0, 1 << 20) % (margin + 1)
    lengths = lengths.at[giver].add(-moved).at[taker].add(moved)
    members = jnp.searchsorted(jnp.cumsum(lengths), jnp.arange(rows * top), side="right").astype(jnp.int32)
    grid = members.reshape(top, rows).T
    grid = grid[jax.random.permutation(jax.random.fold_in(own, 1), rows)]
    rotation = jax.random.randint(jax.random.fold_in(own, 2), (rows, 1), 0, top)
    return jnp.take_along_axis(grid, (jnp.arange(top)[None, :] + rotation) % top, axis=1)


def portions_of(number_of, total, bound, slope, full):
    weights = [(1 << 20) // math.isqrt(standing ** slope) + 1 for standing in range(1, number_of + 1)]
    largest = bound if full else min(bound, max(-(-total // number_of), total * weights[0] // sum(weights)))
    least = 1 if total - largest >= number_of - 1 else 0
    holding, rest = [largest] + [least] * (number_of - 1), total - largest - least * (number_of - 1)
    while rest > 0:
        movable = [i for i in range(1, number_of) if holding[i] < largest] or [i for i in range(1, number_of) if holding[i] < bound]
        mass, budget = sum([weights[i] for i in movable]), rest
        for i in movable:
            more = min(bound - holding[i], max(1, budget * weights[i] // mass), rest)
            holding[i] = holding[i] + more
            rest = rest - more
    return np.array(holding)


def scatter_about(own_key, shape, scale, most, pieces=(), kind=jnp.bfloat16):
    level = block_scale(own_key, shape, pieces, -0.22, 0.18) if pieces else 1.0
    entries = jax.random.normal(own_key, shape, jnp.float32) * scale * level
    return jnp.minimum(jnp.maximum(entries, -most), most).astype(kind)


def setup_inputs(seed: int = 0) -> dict:
    seeds = jax.random.split(jax.random.key(seed), 11)
    hidden_in = draw_hidden_in(jax.random.fold_in(seeds[10], 71), 0)
    queries = draw_queries(jax.random.fold_in(seeds[10], 71), 0)
    rotated_key_value = draw_rotated_key_value(jax.random.fold_in(seeds[10], 71), 0)
    sink_logit_table = jnp.clip(jax.random.uniform(seeds[3], (QUERY_HEADS,), jnp.float32, -2.0, 2.0) * block_scale(seeds[3], (QUERY_HEADS,), ((0, 2),), -0.4, 0.0), -2.0, 2.0)
    out_proj = scatter_about(seeds[4], (QUERY_HEADS * HEAD_SIZE, D), (QUERY_HEADS * HEAD_SIZE) ** -0.5, 0.125, ((0, 2), (1, 16)))
    norm_gain = jnp.clip(1.0 + 0.18 * jax.random.normal(seeds[5], (D,), jnp.float32), 0.1, 1.9)
    expert_in = scatter_about(seeds[6], (EXPERTS, 2, D, FF), D ** -0.5, 0.15625, ((0, 16), (3, 2)))
    expert_out = scatter_about(seeds[7], (EXPERTS, FF, D), FF ** -0.5, 0.15625, ((0, 16), (1, 2)))
    routes_keys = jax.random.split(jax.random.fold_in(seeds[8], 1), TOKEN_TOTAL // TOK_DEV)
    routes_turns = jax.random.permutation(jax.random.fold_in(seeds[8], 3), TOKEN_TOTAL // TOK_DEV)
    routes = jax.vmap(lambda own, number: shared_out(jax.random.fold_in(seeds[8], 2), own, number, TOK_DEV, EXPERTS, TOP, CAP, 2))(routes_keys, routes_turns).reshape((TOKEN_TOTAL, TOP))
    route_scores = jnp.clip(jnp.exp(math.log(1.0) - 2.9957323 * jax.random.uniform(seeds[9], (TOKEN_TOTAL, TOP), jnp.float32) ** block_scale(seeds[9], (TOKEN_TOTAL, TOP), ((0, 16),), -0.2, 0.2)), 0.05, 1.0)
    return dict(hidden_in=hidden_in, queries=queries, rotated_key_value=rotated_key_value, sink_logit_table=sink_logit_table, out_proj=out_proj, norm_gain=norm_gain, expert_in=expert_in, expert_out=expert_out, routes=routes, route_scores=route_scores)


def attend(query_block, key_blk, value_blk, inside, sink_row_block, factor):
    score = jnp.einsum('rgqd,sgd->gqrs', query_block.astype(jnp.float32), key_blk.astype(jnp.float32)) * factor
    masked = jnp.where(inside, score, -1e+30)
    top_score = jnp.maximum(lax.optimization_barrier(jnp.max(masked, -1)), sink_row_block[:, :, None])
    expvals = jnp.where(inside, jnp.exp(score - top_score[..., None]), 0.0)
    denominator = lax.optimization_barrier(jnp.sum(expvals, -1)) + jnp.exp(sink_row_block[:, :, None] - top_score)
    probs = (expvals / denominator[..., None]).astype(jnp.bfloat16)
    mixed = jnp.einsum('gqrs,sgd->rgqd', probs.astype(jnp.float32), value_blk.astype(jnp.float32))
    return mixed.astype(jnp.bfloat16)

def reference(hidden_in, queries, rotated_key_value, sink_logit_table, out_proj, norm_gain, expert_in, expert_out, routes, route_scores):
    factor = HEAD_SIZE ** (-0.5)
    queries_per_group = QUERY_HEADS // KEY_VALUE_HEADS
    block_row_count = TOK_DEV * math.gcd(N_CTX, max(1, 512 // TOK_DEV))
    key_value_padding = jnp.concatenate([jnp.zeros((WINDOW_KEYS, KEY_VALUE_HEADS, 2 * HEAD_SIZE), jnp.bfloat16), rotated_key_value], 0)
    sink_row_block = sink_logit_table.reshape(KEY_VALUE_HEADS, queries_per_group)

    def attend_block(block_id):
        start_shift = block_id * block_row_count
        query_block = lax.dynamic_slice_in_dim(queries, start_shift, block_row_count, 0).reshape(block_row_count, KEY_VALUE_HEADS, queries_per_group, HEAD_SIZE)
        kv_blk = lax.dynamic_slice_in_dim(key_value_padding, start_shift, block_row_count + WINDOW_KEYS, 0)
        query_pos = start_shift + jnp.arange(block_row_count, dtype=jnp.int32)[:, None]
        key_pos = start_shift - WINDOW_KEYS + jnp.arange(block_row_count + WINDOW_KEYS, dtype=jnp.int32)[None, :]
        inside = (key_pos <= query_pos) & (key_pos > query_pos - WINDOW_KEYS) & (key_pos >= 0)
        mixed = attend(query_block, kv_blk[..., :HEAD_SIZE], kv_blk[..., HEAD_SIZE:], inside, sink_row_block, factor)
        return mixed.reshape(block_row_count, QUERY_HEADS * HEAD_SIZE)
    attended = lax.map(attend_block, jnp.arange(TOKEN_TOTAL // block_row_count, dtype=jnp.int32)).reshape(TOKEN_TOTAL, QUERY_HEADS * HEAD_SIZE)
    residual = hidden_in.astype(jnp.float32) + jnp.dot(attended, out_proj, preferred_element_type=jnp.float32)
    mean_sq = lax.optimization_barrier(jnp.mean(residual * residual, -1, keepdims=True))
    normed = (residual * lax.rsqrt(mean_sq + 1e-05) * norm_gain).astype(jnp.bfloat16)
    local_routes = routes.reshape(N_CTX, TOK_DEV, TOP)
    expert_ids = jnp.arange(EXPERTS, dtype=jnp.int32)
    onehot = (local_routes[..., None] == expert_ids).astype(jnp.int32)
    per_tok = lax.optimization_barrier(jnp.sum(onehot, 2))
    before = jnp.cumsum(per_tok, axis=1) - per_tok
    slot_ids = lax.optimization_barrier(jnp.sum(onehot * before[:, :, None, :], -1))
    weights = (route_scores / lax.optimization_barrier(jnp.sum(route_scores, -1, keepdims=True))).reshape(N_CTX, TOK_DEV, TOP)
    source_ids = jnp.broadcast_to(jnp.arange(N_CTX, dtype=jnp.int32)[:, None, None], local_routes.shape)
    token_ids = jnp.broadcast_to(jnp.arange(TOK_DEV, dtype=jnp.int32)[None, :, None], local_routes.shape)
    slot_table = jnp.full((EXPERTS, N_CTX, CAP), TOK_DEV, jnp.int32).at[local_routes, source_ids, slot_ids].set(token_ids)
    slot_weights = jnp.zeros((EXPERTS, N_CTX, CAP), jnp.float32).at[local_routes, source_ids, slot_ids].set(weights)
    normed_pad = jnp.concatenate([normed.reshape(N_CTX, TOK_DEV, D), jnp.zeros((N_CTX, 1, D), jnp.bfloat16)], 1)
    source_rows = jnp.arange(N_CTX, dtype=jnp.int32)[:, None]
    quarter = FF // N_TP

    def expert(running, expert_data):
        table, slot_w, w_in, w_out = expert_data
        row_data = normed_pad[source_rows, table].reshape(N_CTX * CAP, D)
        summed = jnp.zeros((N_CTX * CAP, D), jnp.float32)
        for quarter_id in range(N_TP):
            lower = quarter_id * quarter
            gate_vals = jnp.dot(row_data, w_in[0, :, lower:lower + quarter], preferred_element_type=jnp.float32)
            up_vals = jnp.dot(row_data, w_in[1, :, lower:lower + quarter], preferred_element_type=jnp.float32)
            activated = ((up_vals + 1.0) * gate_vals * jax.nn.sigmoid(1.702 * gate_vals)).astype(jnp.bfloat16)
            partial_value = jnp.dot(activated, w_out[lower:lower + quarter], preferred_element_type=jnp.float32).astype(jnp.bfloat16)
            partial_value = lax.optimization_barrier(partial_value)
            summed = summed + partial_value.astype(jnp.float32)
        result = summed.astype(jnp.bfloat16)
        result = lax.optimization_barrier(result).reshape(N_CTX, CAP, D)
        running = running.at[source_rows, table].add(slot_w[..., None] * result.astype(jnp.float32))
        return (running, None)
    running, _ = lax.scan(expert, jnp.zeros((N_CTX, TOK_DEV + 1, D), jnp.float32), (slot_table, slot_weights, expert_in, expert_out))
    moe_sum = running[:, :TOK_DEV].reshape(TOKEN_TOTAL, D)
    return (residual + moe_sum).astype(jnp.bfloat16)
```

```python
import jax
import jax.numpy as jnp
from jax import lax
from jax.sharding import PartitionSpec as P

WINDOW_KEYS = 128


def shifted(value, axis, steps):
    count = lax.axis_size(axis)
    first, last = (max(0, -steps), min(count, count - steps))
    return lax.ppermute(value, axis, [(source, source + steps) for source in range(first, last)])


def attend(query_block, key_blk, value_blk, inside, sink_row_block, factor):
    score = (
        jnp.einsum("rgqd,sgd->gqrs", query_block, key_blk, preferred_element_type=jnp.float32)
        * factor
    )
    masked = jnp.where(inside, score, -1e30)
    top_score = jnp.maximum(jnp.max(masked, -1), sink_row_block[:, :, None])
    expvals = jnp.where(inside, jnp.exp(score - top_score[..., None]), 0.0)
    denominator = jnp.sum(expvals, -1) + jnp.exp(sink_row_block[:, :, None] - top_score)
    probs = (expvals / denominator[..., None]).astype(jnp.bfloat16)
    mixed = jnp.einsum("gqrs,sgd->rgqd", probs, value_blk, preferred_element_type=jnp.float32)
    return mixed.astype(jnp.bfloat16)


def dense_experts(residual, normed, expert_in, expert_out, routes, weights):
    experts = lax.axis_size("ctx")
    chosen = routes[:, :, None] == jnp.arange(experts, dtype=jnp.int32)
    spread = jnp.sum(jnp.where(chosen, weights[:, :, None], 0.0), 1)
    every = lax.all_gather(spread, "ctx", axis=0, tiled=True)
    mine = lax.dynamic_slice_in_dim(every, lax.axis_index("ctx"), 1, 1)
    wide = lax.all_gather(normed, "tp", axis=1, tiled=True)
    row_data = lax.all_gather(wide, "ctx", axis=0, tiled=True)
    gate_vals = jnp.dot(row_data, expert_in[0, 0], preferred_element_type=jnp.float32)
    up_vals = jnp.dot(row_data, expert_in[0, 1], preferred_element_type=jnp.float32)
    activated = ((up_vals + 1.0) * gate_vals * jax.nn.sigmoid(1.702 * gate_vals)).astype(
        jnp.bfloat16
    )
    result = jnp.dot(activated, expert_out[0], preferred_element_type=jnp.float32)
    result = jnp.where(mine != 0.0, result * mine, 0.0).astype(jnp.bfloat16)
    halves = lax.psum_scatter(result, "tp", scatter_dimension=1, tiled=True)
    total = lax.psum_scatter(halves, "ctx", scatter_dimension=0, tiled=True)
    return (residual + total.astype(jnp.float32)).astype(jnp.bfloat16)


def body(
    hidden_in,
    queries,
    rotated_key_value,
    sink_logit_table,
    out_proj,
    norm_gain,
    expert_in,
    expert_out,
    routes,
    route_scores,
):
    tok_rows = hidden_in.shape[0]
    kv_heads = rotated_key_value.shape[1]
    head_dim = rotated_key_value.shape[2] // 2
    q_heads = sink_logit_table.shape[0]
    queries_per_group = q_heads // kv_heads
    factor = head_dim ** (-0.5)
    sink_row_block = sink_logit_table.reshape(kv_heads, queries_per_group)
    earlier = shifted(rotated_key_value, "ctx", 1)
    keys_all = jnp.concatenate([earlier, rotated_key_value], 0)
    first_pos = lax.axis_index("ctx") * tok_rows
    block_row_count = min(512, tok_rows)
    query_block = queries.reshape(block_row_count, kv_heads, queries_per_group, head_dim)
    query_pos = first_pos + 0 + jnp.arange(block_row_count, dtype=jnp.int32)[:, None]
    key_pos = (
        first_pos
        + 0
        - WINDOW_KEYS
        + jnp.arange(block_row_count + WINDOW_KEYS, dtype=jnp.int32)[None, :]
    )
    inside = (key_pos <= query_pos) & (key_pos > query_pos - WINDOW_KEYS) & (key_pos >= 0)
    mixed = attend(
        query_block,
        keys_all[..., :head_dim],
        keys_all[..., head_dim:],
        inside,
        sink_row_block,
        factor,
    )
    outputs = mixed.reshape(block_row_count, q_heads * head_dim)
    head_partial = jnp.dot(
        outputs,
        lax.all_gather(out_proj, "ctx", axis=1, tiled=True),
        preferred_element_type=jnp.float32,
    )
    d_model = head_partial.shape[1]
    residual = hidden_in.astype(jnp.float32) + lax.psum_scatter(
        head_partial.astype(jnp.bfloat16), "tp", scatter_dimension=1, tiled=True
    ).astype(jnp.float32)
    square_total = lax.psum(jnp.sum(residual * residual, -1), "tp")
    normed = (residual * lax.rsqrt(square_total[:, None] / d_model + 1e-05) * norm_gain).astype(
        jnp.bfloat16
    )
    ctx_count = lax.axis_size("ctx")
    weights = route_scores / jnp.sum(route_scores, -1, keepdims=True)
    if ctx_count <= 16 and expert_in.shape[0] == 1:
        return dense_experts(residual, normed, expert_in, expert_out, routes, weights)
    tp_count = lax.axis_size("tp")
    top_count = routes.shape[1]
    experts = ctx_count * expert_in.shape[0]
    capacity = max(2, min(tok_rows, 3 * top_count * tok_rows // experts))
    quarter_w = d_model // tp_count
    onehot = (routes[:, :, None] == jnp.arange(experts, dtype=jnp.int32)).astype(jnp.int32)
    per_tok = jnp.sum(onehot, 1)
    before = jnp.cumsum(per_tok, axis=0) - per_tok
    slot_ids = jnp.sum(onehot * before[:, None, :], -1)
    flat_index = (routes * capacity + slot_ids).reshape(-1)
    full_data = lax.all_gather(normed, "tp", axis=1, tiled=True)
    row_width = full_data.shape[1]
    spread = jnp.broadcast_to(full_data[:, None, :], (tok_rows, top_count, row_width)).reshape(
        -1, row_width
    )
    outbox = jnp.zeros((experts * capacity, row_width), jnp.bfloat16).at[flat_index].set(spread)
    arrived = lax.all_to_all(
        outbox.reshape(ctx_count, 1, capacity, row_width),
        "ctx",
        split_axis=0,
        concat_axis=1,
        tiled=True,
    )
    leading = arrived.shape[:3]
    row_data = arrived.reshape(-1, d_model)
    gate_vals = jnp.dot(row_data, expert_in[0, 0], preferred_element_type=jnp.float32)
    up_vals = jnp.dot(row_data, expert_in[0, 1], preferred_element_type=jnp.float32)
    activated = ((up_vals + 1.0) * gate_vals * jax.nn.sigmoid(1.702 * gate_vals)).astype(
        jnp.bfloat16
    )
    partial_value = jnp.dot(activated, expert_out[0], preferred_element_type=jnp.float32).astype(
        jnp.bfloat16
    )
    result = partial_value.reshape(leading + (d_model,))
    returned = lax.all_to_all(result, "ctx", split_axis=1, concat_axis=0, tiled=True)
    picked = returned.reshape(-1, d_model)[flat_index].reshape(tok_rows, top_count, d_model)
    expert_result = lax.psum_scatter(
        picked.astype(jnp.float32).astype(jnp.bfloat16), "tp", scatter_dimension=2, tiled=True
    )
    moe_sum = jnp.zeros((tok_rows, quarter_w), jnp.float32)
    for member in range(top_count):
        moe_sum = moe_sum + weights[:, member : member + 1] * expert_result[:, member].astype(
            jnp.float32
        )
    return (residual + moe_sum).astype(jnp.bfloat16)


def solution(mesh):
    in_specs = (
        P("ctx", "tp"),
        P("ctx", "tp"),
        P("ctx", "tp", None),
        P("tp"),
        P("tp", "ctx"),
        P("tp"),
        P("ctx", None, None, "tp"),
        P("ctx", "tp", None),
        P("ctx", None),
        P("ctx", None),
    )
    out_specs = P("ctx", "tp")
    return jax.shard_map(body, mesh=mesh, in_specs=in_specs, out_specs=out_specs, check_vma=False)
```

```python
import jax
import jax.numpy as jnp
from jax import lax
from jax.experimental import pallas as pl
from jax.experimental.pallas import tpu as pltpu
from jax.sharding import PartitionSpec as P

WINDOW_KEYS = 128


def shifted(value, axis, steps):
    count = lax.axis_size(axis)
    first, last = (max(0, -steps), min(count, count - steps))
    return lax.ppermute(value, axis, [(source, source + steps) for source in range(first, last)])


def attend(query_block, key_blk, value_blk, inside, sink_row_block, factor):
    score = (
        jnp.einsum("rgqd,sgd->gqrs", query_block, key_blk, preferred_element_type=jnp.float32)
        * factor
    )
    masked = jnp.where(inside, score, -1e30)
    top_score = jnp.maximum(jnp.max(masked, -1), sink_row_block[:, :, None])
    expvals = jnp.where(inside, jnp.exp(score - top_score[..., None]), 0.0)
    denominator = jnp.sum(expvals, -1) + jnp.exp(sink_row_block[:, :, None] - top_score)
    probs = (expvals / denominator[..., None]).astype(jnp.bfloat16)
    mixed = jnp.einsum("gqrs,sgd->rgqd", probs, value_blk, preferred_element_type=jnp.float32)
    return mixed.astype(jnp.bfloat16)


def expert_kernel(
    normed_ref, mine_ref, residual_ref, w_in_hbm, w_out_hbm, out_ref,
    full, part, w_in, w_out, act, from_core, from_two, from_one, from_z,
    load_sem, own_sem,
    gz_send, gz_recv, g1_send, g1_recv, g2_send, g2_recv, g3_send, g3_recv,
    rc_send, rc_recv, r2_send, r2_recv, r1_send, r1_recv, rz_send, rz_recv,
):
    ctx, x = lax.axis_index("ctx"), lax.axis_index("tp")
    z, y, c = ctx // 4, (ctx // 2) % 2, ctx % 2
    rows = normed_ref.shape[0]
    half = rows // 2
    width = normed_ref.shape[1]
    there = [z, z + 1 - 2 * (z % 2), z + 2 - 4 * (z // 2), 3 - z]

    def place(z_at, y_at, c_at):
        return z_at * 4 + y_at * 2 + c_at

    core_dev, y_dev, x_dev = (place(z, y, 1 - c), x), (place(z, 1 - y, c), x), (ctx, 1 - x)
    z_devs = [None] + [(place(there[o], y, c), x) for o in range(1, 4)]
    first_dev, second_dev = (y_dev, x_dev), (x_dev, y_dev)

    def span(z_at, y_at, c_at, chunk):
        return pl.ds(pl.multiple_of(place(z_at, y_at, c_at) * rows + chunk * half, half), half)

    def block(z_at, y_at, c_at):
        return pl.ds(pl.multiple_of(place(z_at, y_at, c_at) * rows, rows), rows)

    def remote(src, dst, send, recv, device):
        return pltpu.make_async_remote_copy(
            src_ref=src, dst_ref=dst, send_sem=send, recv_sem=recv,
            device_id=device, device_id_type=pl.DeviceIdType.MESH,
        )

    loads = [
        pltpu.make_async_copy(w_in_hbm, w_in, load_sem.at[0]),
        pltpu.make_async_copy(w_out_hbm, w_out, load_sem.at[1]),
    ]
    for load in loads:
        load.start()
    barrier = pltpu.get_barrier_semaphore()
    peers = [core_dev, y_dev, x_dev] + z_devs[1:]
    for peer in peers:
        pl.semaphore_signal(barrier, inc=1, device_id=peer, device_id_type=pl.DeviceIdType.MESH)
    pl.semaphore_wait(barrier, len(peers))

    def piece(chunk, o, one, two, core):
        y_at = y if (one if chunk == 0 else two) == 0 else 1 - y
        x_at = x if (two if chunk == 0 else one) == 0 else 1 - x
        c_at = c if core == 0 else 1 - c
        return full.at[x_at, span(there[o], y_at, c_at, chunk)]

    sends = []

    def send(src, dst, s_sem, r_sem, device):
        copy = remote(src, dst, s_sem, r_sem, device)
        copy.start()
        sends.append(copy)

    own = normed_ref
    own_copies = []
    for chunk in range(2):
        src = own.at[pl.ds(chunk * half, half)]
        dst = piece(chunk, 0, 0, 0, 0)
        for o in (3, 2, 1):
            send(src, dst, gz_send.at[chunk, o], gz_recv.at[chunk, o], z_devs[o])
        keep = pltpu.make_async_copy(src, dst, own_sem.at[chunk])
        keep.start()
        own_copies.append(keep)

    def pass_on(chunk, o, one, two):
        src = own.at[pl.ds(chunk * half, half)] if (o, one, two) == (0, 0, 0) else piece(chunk, o, one, two, 0)
        dst = piece(chunk, o, one, two, 0)
        if one == 0 and two == 0:
            send(src, dst, g1_send.at[chunk, o], g1_recv.at[chunk, o], first_dev[chunk])
        if two == 0:
            send(src, dst, g2_send.at[chunk, o, one], g2_recv.at[chunk, o, one], second_dev[chunk])
        send(src, dst, g3_send.at[chunk, o, one, two], g3_recv.at[chunk, o, one, two], core_dev)

    def arrive(dst, s_sem, r_sem):
        remote(dst, dst, s_sem, r_sem, core_dev).wait_recv()

    def gather(o):
        for chunk in range(2):
            if o:
                arrive(piece(chunk, o, 0, 0, 0), gz_send.at[chunk, o], gz_recv.at[chunk, o])
            pass_on(chunk, o, 0, 0)
        for chunk in range(2):
            arrive(piece(chunk, o, 1, 0, 0), g1_send.at[chunk, o], g1_recv.at[chunk, o])
            pass_on(chunk, o, 1, 0)
        for one in range(2):
            for chunk in range(2):
                arrive(piece(chunk, o, one, 1, 0), g2_send.at[chunk, o, one], g2_recv.at[chunk, o, one])
                pass_on(chunk, o, one, 1)

    def gather_core(o):
        for chunk in range(2):
            for one in range(2):
                for two in range(2):
                    arrive(
                        piece(chunk, o, one, two, 1),
                        g3_send.at[chunk, o, one, two],
                        g3_recv.at[chunk, o, one, two],
                    )

    group = 4 * rows

    def compute(o):
        base = pl.multiple_of(there[o] * group, group)
        near = pl.ds(base, group)
        tile = 256

        @pl.loop(0, width // tile)
        def _(step):
            cols = pl.ds(pl.multiple_of(step * tile, tile), tile)

            def project(which):
                return jnp.dot(
                    full[0, near], w_in[which, pl.ds(0, width), cols], preferred_element_type=jnp.float32
                ) + jnp.dot(
                    full[1, near], w_in[which, pl.ds(width, width), cols], preferred_element_type=jnp.float32
                )

            gate, up = project(0), project(1)
            act[:, cols] = ((up + 1.0) * gate * jax.nn.sigmoid(1.702 * gate)).astype(jnp.bfloat16)

        for at in range(2):

            @pl.loop(0, width // tile)
            def _(step):
                start = pl.multiple_of(step * tile, tile)
                cols = pl.ds(start, tile)
                wide = pl.ds(pl.multiple_of(at * width + step * tile, tile), tile)
                value = jnp.dot(act[...], w_out[:, wide], preferred_element_type=jnp.float32)
                part[at, near, cols] = (value * mine_ref[near]).astype(jnp.bfloat16)

        for x_at in range(2):
            for y_at in range(2):
                send(
                    part.at[x_at, block(there[o], y_at, 1 - c)], from_core.at[o, x_at, y_at],
                    rc_send.at[o, x_at, y_at], rc_recv.at[o, x_at, y_at], core_dev,
                )

    def add(x_at, where, ref):
        part[x_at, where] = (
            part[x_at, where].astype(jnp.float32) + ref[...].astype(jnp.float32)
        ).astype(jnp.bfloat16)

    def reduce_core(o):
        for x_at in range(2):
            for y_at in range(2):
                got = from_core.at[o, x_at, y_at]
                arrive(got, rc_send.at[o, x_at, y_at], rc_recv.at[o, x_at, y_at])
                add(x_at, block(there[o], y_at, c), got)
        for k in range(2):
            send(
                part.at[1 - x, span(there[o], k, c, 0)], from_two.at[0, o, k],
                r2_send.at[0, o, k], r2_recv.at[0, o, k], x_dev,
            )
            send(
                part.at[k, span(there[o], 1 - y, c, 1)], from_two.at[1, o, k],
                r2_send.at[1, o, k], r2_recv.at[1, o, k], y_dev,
            )

    def reduce_two(o):
        for k in range(2):
            for chunk in range(2):
                got = from_two.at[chunk, o, k]
                arrive(got, r2_send.at[chunk, o, k], r2_recv.at[chunk, o, k])
                if chunk == 0:
                    add(x, span(there[o], k, c, 0), got)
                else:
                    add(k, span(there[o], y, c, 1), got)
        send(
            part.at[x, span(there[o], 1 - y, c, 0)], from_one.at[0, o],
            r1_send.at[0, o], r1_recv.at[0, o], y_dev,
        )
        send(
            part.at[1 - x, span(there[o], y, c, 1)], from_one.at[1, o],
            r1_send.at[1, o], r1_recv.at[1, o], x_dev,
        )

    def reduce_one(o):
        for chunk in range(2):
            got = from_one.at[chunk, o]
            arrive(got, r1_send.at[chunk, o], r1_recv.at[chunk, o])
            add(x, span(there[o], y, c, chunk), got)
            if o:
                send(
                    part.at[x, span(there[o], y, c, chunk)], from_z.at[o, chunk],
                    rz_send.at[o, chunk], rz_recv.at[o, chunk], z_devs[o],
                )

    gather(0)
    for keep in own_copies:
        keep.wait()
    for load in loads:
        load.wait()
    gather_core(0)
    compute(0)
    gather(1)
    gather_core(1)
    compute(1)
    reduce_core(0)
    gather(2)
    gather_core(2)
    compute(2)
    reduce_core(1)
    reduce_two(0)
    gather(3)
    gather_core(3)
    compute(3)
    reduce_core(2)
    reduce_two(1)
    reduce_one(0)
    reduce_core(3)
    reduce_two(2)
    reduce_one(1)
    reduce_two(3)
    reduce_one(2)
    reduce_one(3)
    for chunk in range(2):
        mine_rows = pl.ds(chunk * half, half)
        total = residual_ref[mine_rows] + part[x, span(z, y, c, chunk)].astype(jnp.float32)
        for o in range(1, 4):
            arrive(from_z.at[o, chunk], rz_send.at[o, chunk], rz_recv.at[o, chunk])
            total = total + from_z[o, chunk].astype(jnp.float32)
        out_ref[mine_rows] = total.astype(jnp.bfloat16)
    for copy in sends:
        copy.wait_send()


def dense_experts(residual, normed, expert_in, expert_out, routes, weights):
    experts = lax.axis_size("ctx")
    rows, width = normed.shape
    chosen = routes[:, :, None] == jnp.arange(experts, dtype=jnp.int32)
    spread = jnp.sum(jnp.where(chosen, weights[:, :, None], 0.0), 1)
    every = lax.all_gather(spread, "ctx", axis=0, tiled=True)
    mine = lax.dynamic_slice_in_dim(every, lax.axis_index("ctx"), 1, 1)
    dma = pltpu.SemaphoreType.DMA
    bf16 = jnp.bfloat16
    vmem = pl.BlockSpec(memory_space=pltpu.VMEM)
    total = experts * rows
    hidden = expert_in.shape[3]
    flops = 2 * total * hidden * width * 2 * 3
    return pl.pallas_call(
        expert_kernel,
        out_shape=jax.ShapeDtypeStruct((rows, width), bf16),
        in_specs=[vmem] * 3 + [pl.BlockSpec(memory_space=pl.ANY)] * 2,
        out_specs=vmem,
        scratch_shapes=[
            pltpu.VMEM((2, total, width), bf16),
            pltpu.VMEM((2, total, width), bf16),
            pltpu.VMEM((2, 2 * width, hidden), bf16),
            pltpu.VMEM((hidden, 2 * width), bf16),
            pltpu.VMEM((4 * rows, hidden), bf16),
            pltpu.VMEM((4, 2, 2, rows, width), bf16),
            pltpu.VMEM((2, 4, 2, rows // 2, width), bf16),
            pltpu.VMEM((2, 4, rows // 2, width), bf16),
            pltpu.VMEM((4, 2, rows // 2, width), bf16),
            dma((2,)),
            dma((2,)),
        ]
        + [dma((2, 4))] * 4
        + [dma((2, 4, 2))] * 2
        + [dma((2, 4, 2, 2))] * 2
        + [dma((4, 2, 2))] * 2
        + [dma((2, 4, 2))] * 2
        + [dma((2, 4))] * 2
        + [dma((4, 2))] * 2,
        compiler_params=pltpu.CompilerParams(
            collective_id=1, has_side_effects=True, vmem_limit_bytes=50 * 2**20
        ),
        cost_estimate=pl.CostEstimate(flops=flops, bytes_accessed=8 * 2**20, transcendentals=0),
    )(normed, mine, residual, expert_in[0], expert_out[0])


def body(
    hidden_in,
    queries,
    rotated_key_value,
    sink_logit_table,
    out_proj,
    norm_gain,
    expert_in,
    expert_out,
    routes,
    route_scores,
):
    tok_rows = hidden_in.shape[0]
    kv_heads = rotated_key_value.shape[1]
    head_dim = rotated_key_value.shape[2] // 2
    q_heads = sink_logit_table.shape[0]
    queries_per_group = q_heads // kv_heads
    factor = head_dim ** (-0.5)
    sink_row_block = sink_logit_table.reshape(kv_heads, queries_per_group)
    earlier = shifted(rotated_key_value, "ctx", 1)
    keys_all = jnp.concatenate([earlier, rotated_key_value], 0)
    first_pos = lax.axis_index("ctx") * tok_rows
    block_row_count = min(512, tok_rows)
    query_block = queries.reshape(block_row_count, kv_heads, queries_per_group, head_dim)
    query_pos = first_pos + 0 + jnp.arange(block_row_count, dtype=jnp.int32)[:, None]
    key_pos = (
        first_pos
        + 0
        - WINDOW_KEYS
        + jnp.arange(block_row_count + WINDOW_KEYS, dtype=jnp.int32)[None, :]
    )
    inside = (key_pos <= query_pos) & (key_pos > query_pos - WINDOW_KEYS) & (key_pos >= 0)
    mixed = attend(
        query_block,
        keys_all[..., :head_dim],
        keys_all[..., head_dim:],
        inside,
        sink_row_block,
        factor,
    )
    outputs = mixed.reshape(block_row_count, q_heads * head_dim)
    head_partial = jnp.dot(
        outputs,
        lax.all_gather(out_proj, "ctx", axis=1, tiled=True),
        preferred_element_type=jnp.float32,
    )
    d_model = head_partial.shape[1]
    residual = hidden_in.astype(jnp.float32) + lax.psum_scatter(
        head_partial.astype(jnp.bfloat16), "tp", scatter_dimension=1, tiled=True
    ).astype(jnp.float32)
    square_total = lax.psum(jnp.sum(residual * residual, -1), "tp")
    normed = (residual * lax.rsqrt(square_total[:, None] / d_model + 1e-05) * norm_gain).astype(
        jnp.bfloat16
    )
    ctx_count = lax.axis_size("ctx")
    weights = route_scores / jnp.sum(route_scores, -1, keepdims=True)
    if ctx_count == 16 and lax.axis_size("tp") == 2 and expert_in.shape[0] == 1:
        return dense_experts(residual, normed, expert_in, expert_out, routes, weights)
    tp_count = lax.axis_size("tp")
    top_count = routes.shape[1]
    experts = ctx_count * expert_in.shape[0]
    capacity = max(2, min(tok_rows, 3 * top_count * tok_rows // experts))
    quarter_w = d_model // tp_count
    onehot = (routes[:, :, None] == jnp.arange(experts, dtype=jnp.int32)).astype(jnp.int32)
    per_tok = jnp.sum(onehot, 1)
    position = jnp.arange(tok_rows, dtype=jnp.int32)
    earlier_rows = (position[:, None] > position[None, :]).astype(jnp.bfloat16)
    before = jnp.dot(
        earlier_rows, per_tok.astype(jnp.bfloat16), preferred_element_type=jnp.float32
    ).astype(jnp.int32)
    slot_ids = jnp.sum(onehot * before[:, None, :], -1)
    flat_index = (routes * capacity + slot_ids).reshape(-1)
    full_data = lax.all_gather(normed, "tp", axis=1, tiled=True)
    row_width = full_data.shape[1]
    spread = jnp.broadcast_to(full_data[:, None, :], (tok_rows, top_count, row_width)).reshape(
        -1, row_width
    )
    outbox = jnp.zeros((experts * capacity, row_width), jnp.bfloat16).at[flat_index].set(spread)
    arrived = lax.all_to_all(
        outbox.reshape(ctx_count, 1, capacity, row_width),
        "ctx",
        split_axis=0,
        concat_axis=1,
        tiled=True,
    )
    leading = arrived.shape[:3]
    row_data = arrived.reshape(-1, d_model)
    gate_vals = jnp.dot(row_data, expert_in[0, 0], preferred_element_type=jnp.float32)
    up_vals = jnp.dot(row_data, expert_in[0, 1], preferred_element_type=jnp.float32)
    activated = ((up_vals + 1.0) * gate_vals * jax.nn.sigmoid(1.702 * gate_vals)).astype(
        jnp.bfloat16
    )
    partial_value = jnp.dot(activated, expert_out[0], preferred_element_type=jnp.float32).astype(
        jnp.bfloat16
    )
    result = partial_value.reshape(leading + (d_model,))
    returned = lax.all_to_all(result, "ctx", split_axis=1, concat_axis=0, tiled=True)
    picked = returned.reshape(-1, d_model)[flat_index].reshape(tok_rows, top_count, d_model)
    expert_result = lax.psum_scatter(
        picked.astype(jnp.float32).astype(jnp.bfloat16), "tp", scatter_dimension=2, tiled=True
    )
    moe_sum = jnp.zeros((tok_rows, quarter_w), jnp.float32)
    for member in range(top_count):
        moe_sum = moe_sum + weights[:, member : member + 1] * expert_result[:, member].astype(
            jnp.float32
        )
    return (residual + moe_sum).astype(jnp.bfloat16)


def solution(mesh):
    in_specs = (
        P("ctx", "tp"),
        P("ctx", "tp"),
        P("ctx", "tp", None),
        P("tp"),
        P("tp", "ctx"),
        P("tp"),
        P("ctx", None, None, "tp"),
        P("ctx", "tp", None),
        P("ctx", None),
        P("ctx", None),
    )
    out_specs = P("ctx", "tp")
    return jax.shard_map(body, mesh=mesh, in_specs=in_specs, out_specs=out_specs, check_vma=False)
```

```python
import jax
import jax.numpy as jnp
from jax import lax
from jax.experimental import pallas as pl
from jax.experimental.pallas import tpu as pltpu
from jax.sharding import PartitionSpec as P

WINDOW_KEYS = 128


def shifted(value, axis, steps):
    count = lax.axis_size(axis)
    first, last = (max(0, -steps), min(count, count - steps))
    return lax.ppermute(value, axis, [(source, source + steps) for source in range(first, last)])


def attend(query_block, key_blk, value_blk, inside, sink_row_block, factor):
    score = (
        jnp.einsum("rgqd,sgd->gqrs", query_block, key_blk, preferred_element_type=jnp.float32)
        * factor
    )
    masked = jnp.where(inside, score, -1e30)
    top_score = jnp.maximum(jnp.max(masked, -1), sink_row_block[:, :, None])
    expvals = jnp.where(inside, jnp.exp(score - top_score[..., None]), 0.0)
    denominator = jnp.sum(expvals, -1) + jnp.exp(sink_row_block[:, :, None] - top_score)
    probs = (expvals / denominator[..., None]).astype(jnp.bfloat16)
    mixed = jnp.einsum("gqrs,sgd->rgqd", probs, value_blk, preferred_element_type=jnp.float32)
    return mixed.astype(jnp.bfloat16)


def expert_kernel(
    normed_ref, mine_ref, residual_ref, w_in_hbm, w_out_hbm, out_ref,
    full, part, w_in, w_out, act, from_core, from_two, from_one, from_z,
    load_sem, own_sem,
    gz_send, gz_recv, g1_send, g1_recv, g2_send, g2_recv, g3_send, g3_recv,
    rc_send, rc_recv, r2_send, r2_recv, r1_send, r1_recv, rz_send, rz_recv,
):
    ctx, x = lax.axis_index("ctx"), lax.axis_index("tp")
    z, y, c = ctx // 4, (ctx // 2) % 2, ctx % 2
    rows = normed_ref.shape[0]
    half = rows // 2
    width = normed_ref.shape[1]
    there = [z, z + 1 - 2 * (z % 2), z + 2 - 4 * (z // 2), 3 - z]

    def place(z_at, y_at, c_at):
        return z_at * 4 + y_at * 2 + c_at

    core_dev, y_dev, x_dev = (place(z, y, 1 - c), x), (place(z, 1 - y, c), x), (ctx, 1 - x)
    z_devs = [None] + [(place(there[o], y, c), x) for o in range(1, 4)]
    first_dev, second_dev = (y_dev, x_dev), (x_dev, y_dev)

    def span(z_at, y_at, c_at, chunk):
        return pl.ds(pl.multiple_of(place(z_at, y_at, c_at) * rows + chunk * half, half), half)

    def block(z_at, y_at, c_at):
        return pl.ds(pl.multiple_of(place(z_at, y_at, c_at) * rows, rows), rows)

    def remote(src, dst, send, recv, device):
        return pltpu.make_async_remote_copy(
            src_ref=src, dst_ref=dst, send_sem=send, recv_sem=recv,
            device_id=device, device_id_type=pl.DeviceIdType.MESH,
        )

    loads = [
        pltpu.make_async_copy(w_in_hbm, w_in, load_sem.at[0]),
        pltpu.make_async_copy(w_out_hbm, w_out, load_sem.at[1]),
    ]
    for load in loads:
        load.start()
    barrier = pltpu.get_barrier_semaphore()
    peers = [core_dev, y_dev, x_dev] + z_devs[1:]
    for peer in peers:
        pl.semaphore_signal(barrier, inc=1, device_id=peer, device_id_type=pl.DeviceIdType.MESH)
    pl.semaphore_wait(barrier, len(peers))

    def piece(chunk, o, one, two, core):
        y_at = y if (one if chunk == 0 else two) == 0 else 1 - y
        x_at = x if (two if chunk == 0 else one) == 0 else 1 - x
        c_at = c if core == 0 else 1 - c
        return full.at[x_at, span(there[o], y_at, c_at, chunk)]

    sends = []

    def send(src, dst, s_sem, r_sem, device):
        copy = remote(src, dst, s_sem, r_sem, device)
        copy.start()
        sends.append(copy)

    own = normed_ref
    own_copies = []
    for chunk in range(2):
        src = own.at[pl.ds(chunk * half, half)]
        dst = piece(chunk, 0, 0, 0, 0)
        for o in (3, 2, 1):
            send(src, dst, gz_send.at[chunk, o], gz_recv.at[chunk, o], z_devs[o])
        keep = pltpu.make_async_copy(src, dst, own_sem.at[chunk])
        keep.start()
        own_copies.append(keep)

    def pass_on(chunk, o, one, two):
        src = own.at[pl.ds(chunk * half, half)] if (o, one, two) == (0, 0, 0) else piece(chunk, o, one, two, 0)
        dst = piece(chunk, o, one, two, 0)
        if one == 0 and two == 0:
            send(src, dst, g1_send.at[chunk, o], g1_recv.at[chunk, o], first_dev[chunk])
        if two == 0:
            send(src, dst, g2_send.at[chunk, o, one], g2_recv.at[chunk, o, one], second_dev[chunk])
        send(src, dst, g3_send.at[chunk, o, one, two], g3_recv.at[chunk, o, one, two], core_dev)

    def arrive(dst, s_sem, r_sem):
        remote(dst, dst, s_sem, r_sem, core_dev).wait_recv()

    def gather(o):
        for chunk in range(2):
            if o:
                arrive(piece(chunk, o, 0, 0, 0), gz_send.at[chunk, o], gz_recv.at[chunk, o])
            pass_on(chunk, o, 0, 0)
        for chunk in range(2):
            arrive(piece(chunk, o, 1, 0, 0), g1_send.at[chunk, o], g1_recv.at[chunk, o])
            pass_on(chunk, o, 1, 0)
        for one in range(2):
            for chunk in range(2):
                arrive(piece(chunk, o, one, 1, 0), g2_send.at[chunk, o, one], g2_recv.at[chunk, o, one])
                pass_on(chunk, o, one, 1)

    def gather_core(o):
        for chunk in range(2):
            for one in range(2):
                for two in range(2):
                    arrive(
                        piece(chunk, o, one, two, 1),
                        g3_send.at[chunk, o, one, two],
                        g3_recv.at[chunk, o, one, two],
                    )

    group = 4 * rows

    def compute(o):
        base = pl.multiple_of(there[o] * group, group)
        near = pl.ds(base, group)
        tile = 256

        @pl.loop(0, width // tile)
        def _(step):
            cols = pl.ds(pl.multiple_of(step * tile, tile), tile)

            def project(which):
                return jnp.dot(
                    full[0, near], w_in[which, pl.ds(0, width), cols], preferred_element_type=jnp.float32
                ) + jnp.dot(
                    full[1, near], w_in[which, pl.ds(width, width), cols], preferred_element_type=jnp.float32
                )

            gate, up = project(0), project(1)
            act[:, cols] = ((up + 1.0) * gate * jax.nn.sigmoid(1.702 * gate)).astype(jnp.bfloat16)

        for at in range(2):

            @pl.loop(0, width // tile)
            def _(step):
                start = pl.multiple_of(step * tile, tile)
                cols = pl.ds(start, tile)
                wide = pl.ds(pl.multiple_of(at * width + step * tile, tile), tile)
                value = jnp.dot(act[...], w_out[:, wide], preferred_element_type=jnp.float32)
                part[at, near, cols] = (value * mine_ref[near]).astype(jnp.bfloat16)

        for x_at in range(2):
            for y_at in range(2):
                send(
                    part.at[x_at, block(there[o], y_at, 1 - c)], from_core.at[o, x_at, y_at],
                    rc_send.at[o, x_at, y_at], rc_recv.at[o, x_at, y_at], core_dev,
                )

    def add(x_at, where, ref):
        part[x_at, where] = (
            part[x_at, where].astype(jnp.float32) + ref[...].astype(jnp.float32)
        ).astype(jnp.bfloat16)

    def reduce_core(o):
        for x_at in range(2):
            for y_at in range(2):
                got = from_core.at[o, x_at, y_at]
                arrive(got, rc_send.at[o, x_at, y_at], rc_recv.at[o, x_at, y_at])
                add(x_at, block(there[o], y_at, c), got)
        for k in range(2):
            send(
                part.at[1 - x, span(there[o], k, c, 0)], from_two.at[0, o, k],
                r2_send.at[0, o, k], r2_recv.at[0, o, k], x_dev,
            )
            send(
                part.at[k, span(there[o], 1 - y, c, 1)], from_two.at[1, o, k],
                r2_send.at[1, o, k], r2_recv.at[1, o, k], y_dev,
            )

    def reduce_two(o):
        for k in range(2):
            for chunk in range(2):
                got = from_two.at[chunk, o, k]
                arrive(got, r2_send.at[chunk, o, k], r2_recv.at[chunk, o, k])
                if chunk == 0:
                    add(x, span(there[o], k, c, 0), got)
                else:
                    add(k, span(there[o], y, c, 1), got)
        send(
            part.at[x, span(there[o], 1 - y, c, 0)], from_one.at[0, o],
            r1_send.at[0, o], r1_recv.at[0, o], y_dev,
        )
        send(
            part.at[1 - x, span(there[o], y, c, 1)], from_one.at[1, o],
            r1_send.at[1, o], r1_recv.at[1, o], x_dev,
        )

    def reduce_one(o):
        for chunk in range(2):
            got = from_one.at[chunk, o]
            arrive(got, r1_send.at[chunk, o], r1_recv.at[chunk, o])
            add(x, span(there[o], y, c, chunk), got)
            if o:
                send(
                    part.at[x, span(there[o], y, c, chunk)], from_z.at[o, chunk],
                    rz_send.at[o, chunk], rz_recv.at[o, chunk], z_devs[o],
                )

    gather(0)
    for keep in own_copies:
        keep.wait()
    for load in loads:
        load.wait()
    gather_core(0)
    compute(0)
    gather(1)
    gather_core(1)
    compute(1)
    reduce_core(0)
    gather(2)
    gather_core(2)
    compute(2)
    reduce_core(1)
    reduce_two(0)
    gather(3)
    gather_core(3)
    compute(3)
    reduce_core(2)
    reduce_two(1)
    reduce_one(0)
    reduce_core(3)
    reduce_two(2)
    reduce_one(1)
    reduce_two(3)
    reduce_one(2)
    reduce_one(3)
    for chunk in range(2):
        mine_rows = pl.ds(chunk * half, half)
        total = residual_ref[mine_rows] + part[x, span(z, y, c, chunk)].astype(jnp.float32)
        for o in range(1, 4):
            arrive(from_z.at[o, chunk], rz_send.at[o, chunk], rz_recv.at[o, chunk])
            total = total + from_z[o, chunk].astype(jnp.float32)
        out_ref[mine_rows] = total.astype(jnp.bfloat16)
    for copy in sends:
        copy.wait_send()


def front_kernel(
    q_ref, kv_ref, sink_ref, proj_ref, spread_ref, hidden_ref, gain_ref,
    residual_ref, normed_ref, table_ref,
    keys, proj, att, sums, outgoing, incoming, square_out, square_in,
    own_sem, kv_send, kv_recv, x_send, x_recv, s_send, s_recv,
    pz_send, pz_recv, py_send, py_recv, pc_send, pc_recv,
    wz_send, wz_recv, wy_send, wy_recv, wc_send, wc_recv,
):
    ctx, x = lax.axis_index("ctx"), lax.axis_index("tp")
    z, y, c = ctx // 4, (ctx // 2) % 2, ctx % 2
    there = [z, z + 1 - 2 * (z % 2), z + 2 - 4 * (z // 2), 3 - z]
    rows = q_ref.shape[0]
    wide = proj_ref.shape[0]
    count = 16

    def place(z_at, y_at, c_at):
        return z_at * 4 + y_at * 2 + c_at

    core_dev, y_dev, x_dev = (place(z, y, 1 - c), x), (place(z, 1 - y, c), x), (ctx, 1 - x)
    z_devs = [None] + [(place(there[o], y, c), x) for o in range(1, 4)]
    next_dev, last_dev = ((ctx + 1) % count, x), ((ctx + count - 1) % count, x)

    def remote(src, dst, send, recv, device):
        return pltpu.make_async_remote_copy(
            src_ref=src, dst_ref=dst, send_sem=send, recv_sem=recv,
            device_id=device, device_id_type=pl.DeviceIdType.MESH,
        )

    def columns(z_at, y_at, c_at):
        return proj.at[pl.ds(pl.multiple_of(place(z_at, y_at, c_at) * wide, 16), wide)]

    def share(z_at, y_at, c_at):
        return table_ref.at[place(z_at, y_at, c_at)]

    barrier = pltpu.get_barrier_semaphore()
    peers = [core_dev, y_dev, x_dev, next_dev, last_dev] + z_devs[1:]
    for peer in peers:
        pl.semaphore_signal(barrier, inc=1, device_id=peer, device_id_type=pl.DeviceIdType.MESH)
    pl.semaphore_wait(barrier, len(peers))

    sends = []

    def send(src, dst, s_sem, r_sem, device):
        copy = remote(src, dst, s_sem, r_sem, device)
        copy.start()
        sends.append(copy)

    def arrive(dst, s_sem, r_sem):
        remote(dst, dst, s_sem, r_sem, core_dev).wait_recv()

    send(kv_ref, keys.at[pl.ds(0, rows)], kv_send.at[0], kv_recv.at[0], next_dev)
    for o in (3, 2, 1):
        send(proj_ref, columns(z, y, c), pz_send.at[o], pz_recv.at[o], z_devs[o])
        send(spread_ref, share(z, y, c), wz_send.at[o], wz_recv.at[o], z_devs[o])
    keeps = [
        pltpu.make_async_copy(kv_ref, keys.at[pl.ds(rows, rows)], own_sem.at[0]),
        pltpu.make_async_copy(proj_ref, columns(z, y, c), own_sem.at[1]),
        pltpu.make_async_copy(spread_ref, share(z, y, c), own_sem.at[2]),
    ]
    for keep in keeps:
        keep.start()

    def pass_on(o, y_flip):
        y_at = 1 - y if y_flip else y
        own = o == 0 and not y_flip
        src = proj_ref if own else columns(there[o], y_at, c)
        small = spread_ref if own else share(there[o], y_at, c)
        if not y_flip:
            send(src, columns(there[o], y_at, c), py_send.at[o], py_recv.at[o], y_dev)
            send(small, share(there[o], y_at, c), wy_send.at[o], wy_recv.at[o], y_dev)
        send(src, columns(there[o], y_at, c), pc_send.at[o, y_flip], pc_recv.at[o, y_flip], core_dev)
        send(small, share(there[o], y_at, c), wc_send.at[o, y_flip], wc_recv.at[o, y_flip], core_dev)

    def from_line(o):
        if o:
            arrive(columns(there[o], y, c), pz_send.at[o], pz_recv.at[o])
            arrive(share(there[o], y, c), wz_send.at[o], wz_recv.at[o])
        pass_on(o, 0)

    def from_y(o):
        arrive(columns(there[o], 1 - y, c), py_send.at[o], py_recv.at[o])
        arrive(share(there[o], 1 - y, c), wy_send.at[o], wy_recv.at[o])
        pass_on(o, 1)

    def from_core(o):
        for y_flip in range(2):
            y_at = 1 - y if y_flip else y
            arrive(columns(there[o], y_at, 1 - c), pc_send.at[o, y_flip], pc_recv.at[o, y_flip])
            arrive(share(there[o], y_at, 1 - c), wc_send.at[o, y_flip], wc_recv.at[o, y_flip])

    lane = lax.broadcasted_iota(jnp.int32, (rows, 128), 1)
    query_pos = lax.broadcasted_iota(jnp.int32, (rows, 2 * rows), 0) + rows
    key_pos = lax.broadcasted_iota(jnp.int32, (rows, 2 * rows), 1)
    inside = (
        (key_pos <= query_pos)
        & (key_pos > query_pos - WINDOW_KEYS)
        & (key_pos + ctx * rows >= rows)
    )

    def attention(group):
        key_value = keys[:, group * 128 : group * 128 + 128]
        value_key = keys[:, 256 + group * 128 : 256 + group * 128 + 128]

        @pl.loop(0, 4)
        def _(step):
            pair = group * 4 + step
            cols = pl.ds(pl.multiple_of(pair * 128, 128), 128)
            both = q_ref[:, cols]
            mixed = []
            for odd in range(2):
                q = jnp.where((lane >= 64) if odd else (lane < 64), both, jnp.zeros_like(both))
                sink = sink_ref[pair * 2 + odd]
                score = lax.dot_general(
                    q, value_key if odd else key_value, (((1,), (1,)), ((), ())),
                    preferred_element_type=jnp.float32,
                ) * 0.125
                top = jnp.maximum(jnp.max(jnp.where(inside, score, -1e30), -1, keepdims=True), sink)
                vals = jnp.where(inside, jnp.exp(score - top), 0.0)
                under = jnp.sum(vals, -1, keepdims=True) + jnp.exp(sink - top)
                probs = (vals / under).astype(jnp.bfloat16)
                mixed.append(
                    jnp.dot(probs, key_value if odd else value_key, preferred_element_type=jnp.float32)
                )
            att[:, cols] = jnp.where(lane < 64, mixed[0], mixed[1]).astype(jnp.bfloat16)

    span = 4 * wide

    def project(o):
        near = pl.ds(pl.multiple_of(there[o] * span, 16), span)
        value = lax.dot_general(
            att[...], proj[near], (((1,), (1,)), ((), ())), preferred_element_type=jnp.float32
        )
        sums[there[o]] = value
        outgoing[there[o]] = value.astype(jnp.bfloat16)
        slot = there[o] % 2

        @pl.when(there[o] // 2 != x)
        def _():
            remote(
                outgoing.at[there[o]], incoming.at[slot], x_send.at[slot], x_recv.at[slot], x_dev
            ).start()

    from_line(0)
    for keep in keeps:
        keep.wait()
    arrive(keys.at[pl.ds(0, rows)], kv_send.at[0], kv_recv.at[0])
    attention(0)
    from_line(1)
    from_y(0)
    attention(1)
    from_line(2)
    from_y(1)
    from_core(0)
    project(0)
    from_line(3)
    from_y(2)
    from_core(1)
    project(1)
    from_y(3)
    from_core(2)
    project(2)
    from_core(3)
    project(3)
    squares = jnp.zeros((rows, 1), jnp.float32)
    for slot in range(2):
        arrive(incoming.at[slot], x_send.at[slot], x_recv.at[slot])
        cols = pl.ds(slot * span, span)
        value = (
            hidden_ref[:, cols].astype(jnp.float32)
            + (sums[2 * x + slot] + incoming[slot].astype(jnp.float32))
        )
        residual_ref[:, cols] = value
        squares = squares + jnp.sum(value * value, -1, keepdims=True)
    square_out[...] = jnp.broadcast_to(squares, square_out.shape)
    send(square_out, square_in, s_send.at[0], s_recv.at[0], x_dev)
    arrive(square_in, s_send.at[0], s_recv.at[0])
    total = squares + square_in[:, 0:1]
    scale = lax.rsqrt(total / (2 * residual_ref.shape[1]) + 1e-05)
    normed_ref[...] = (residual_ref[...] * scale * gain_ref[...]).astype(jnp.bfloat16)
    for slot in range(2):
        remote(
            outgoing.at[2 * (1 - x) + slot], incoming.at[slot], x_send.at[slot], x_recv.at[slot], x_dev
        ).wait_send()
    for copy in sends:
        copy.wait_send()


def dense_layer(
    hidden_in, queries, rotated_key_value, sink_logit_table, out_proj, norm_gain,
    expert_in, expert_out, routes, route_scores,
):
    rows, width = hidden_in.shape
    heads_width = queries.shape[1]
    experts = lax.axis_size("ctx")
    weights = route_scores / jnp.sum(route_scores, -1, keepdims=True)
    chosen = routes[:, :, None] == jnp.arange(experts, dtype=jnp.int32)
    spread = jnp.sum(jnp.where(chosen, weights[:, :, None], 0.0), 1).T
    key_value = rotated_key_value.reshape(rows, -1)
    value_key = jnp.concatenate([rotated_key_value[..., 64:], rotated_key_value[..., :64]], -1)
    pairs = jnp.concatenate([key_value, value_key.reshape(rows, -1)], 1)
    wide = out_proj.shape[1]
    dma = pltpu.SemaphoreType.DMA
    bf16, f32 = jnp.bfloat16, jnp.float32
    vmem = pl.BlockSpec(memory_space=pltpu.VMEM)
    residual, normed, table = pl.pallas_call(
        front_kernel,
        out_shape=(
            jax.ShapeDtypeStruct((rows, width), f32),
            jax.ShapeDtypeStruct((rows, width), bf16),
            jax.ShapeDtypeStruct((experts, experts, rows), f32),
        ),
        in_specs=[vmem, vmem, pl.BlockSpec(memory_space=pltpu.SMEM)] + [vmem] * 4,
        out_specs=(vmem, vmem, vmem),
        scratch_shapes=[
            pltpu.VMEM((2 * rows, 512), bf16),
            pltpu.VMEM((experts * wide, heads_width), bf16),
            pltpu.VMEM((rows, heads_width), bf16),
            pltpu.VMEM((4, rows, 4 * wide), f32),
            pltpu.VMEM((4, rows, 4 * wide), bf16),
            pltpu.VMEM((2, rows, 4 * wide), bf16),
            pltpu.VMEM((rows, 128), f32),
            pltpu.VMEM((rows, 128), f32),
            dma((3,)), dma((1,)), dma((1,)), dma((2,)), dma((2,)), dma((1,)), dma((1,)),
        ]
        + ([dma((4,))] * 4 + [dma((4, 2))] * 2) * 2,
        compiler_params=pltpu.CompilerParams(
            collective_id=2, has_side_effects=True, vmem_limit_bytes=32 * 2**20
        ),
        cost_estimate=pl.CostEstimate(flops=10**9, bytes_accessed=4 * 2**20, transcendentals=0),
    )(queries, pairs, sink_logit_table, out_proj.T, spread, hidden_in, norm_gain[None, :])
    mine = lax.dynamic_slice_in_dim(table, lax.axis_index("ctx"), 1, 1).reshape(experts * rows, 1)
    return dense_experts(residual, normed, expert_in, expert_out, mine)


def dense_experts(residual, normed, expert_in, expert_out, mine):
    experts = lax.axis_size("ctx")
    rows, width = normed.shape
    dma = pltpu.SemaphoreType.DMA
    bf16 = jnp.bfloat16
    vmem = pl.BlockSpec(memory_space=pltpu.VMEM)
    total = experts * rows
    hidden = expert_in.shape[3]
    flops = 2 * total * hidden * width * 2 * 3
    return pl.pallas_call(
        expert_kernel,
        out_shape=jax.ShapeDtypeStruct((rows, width), bf16),
        in_specs=[vmem] * 3 + [pl.BlockSpec(memory_space=pl.ANY)] * 2,
        out_specs=vmem,
        scratch_shapes=[
            pltpu.VMEM((2, total, width), bf16),
            pltpu.VMEM((2, total, width), bf16),
            pltpu.VMEM((2, 2 * width, hidden), bf16),
            pltpu.VMEM((hidden, 2 * width), bf16),
            pltpu.VMEM((4 * rows, hidden), bf16),
            pltpu.VMEM((4, 2, 2, rows, width), bf16),
            pltpu.VMEM((2, 4, 2, rows // 2, width), bf16),
            pltpu.VMEM((2, 4, rows // 2, width), bf16),
            pltpu.VMEM((4, 2, rows // 2, width), bf16),
            dma((2,)),
            dma((2,)),
        ]
        + [dma((2, 4))] * 4
        + [dma((2, 4, 2))] * 2
        + [dma((2, 4, 2, 2))] * 2
        + [dma((4, 2, 2))] * 2
        + [dma((2, 4, 2))] * 2
        + [dma((2, 4))] * 2
        + [dma((4, 2))] * 2,
        compiler_params=pltpu.CompilerParams(
            collective_id=1, has_side_effects=True, vmem_limit_bytes=50 * 2**20
        ),
        cost_estimate=pl.CostEstimate(flops=flops, bytes_accessed=8 * 2**20, transcendentals=0),
    )(normed, mine, residual, expert_in[0], expert_out[0])


def body(
    hidden_in,
    queries,
    rotated_key_value,
    sink_logit_table,
    out_proj,
    norm_gain,
    expert_in,
    expert_out,
    routes,
    route_scores,
):
    tok_rows = hidden_in.shape[0]
    small = lax.axis_size("ctx") == 16 and lax.axis_size("tp") == 2
    if small and rotated_key_value.shape[1:] == (2, 128) and tok_rows == 128:
        return dense_layer(
            hidden_in, queries, rotated_key_value, sink_logit_table, out_proj, norm_gain,
            expert_in, expert_out, routes, route_scores,
        )
    kv_heads = rotated_key_value.shape[1]
    head_dim = rotated_key_value.shape[2] // 2
    q_heads = sink_logit_table.shape[0]
    queries_per_group = q_heads // kv_heads
    factor = head_dim ** (-0.5)
    sink_row_block = sink_logit_table.reshape(kv_heads, queries_per_group)
    earlier = shifted(rotated_key_value, "ctx", 1)
    keys_all = jnp.concatenate([earlier, rotated_key_value], 0)
    first_pos = lax.axis_index("ctx") * tok_rows
    block_row_count = min(512, tok_rows)
    query_block = queries.reshape(block_row_count, kv_heads, queries_per_group, head_dim)
    query_pos = first_pos + 0 + jnp.arange(block_row_count, dtype=jnp.int32)[:, None]
    key_pos = (
        first_pos
        + 0
        - WINDOW_KEYS
        + jnp.arange(block_row_count + WINDOW_KEYS, dtype=jnp.int32)[None, :]
    )
    inside = (key_pos <= query_pos) & (key_pos > query_pos - WINDOW_KEYS) & (key_pos >= 0)
    mixed = attend(
        query_block,
        keys_all[..., :head_dim],
        keys_all[..., head_dim:],
        inside,
        sink_row_block,
        factor,
    )
    outputs = mixed.reshape(block_row_count, q_heads * head_dim)
    head_partial = jnp.dot(
        outputs,
        lax.all_gather(out_proj, "ctx", axis=1, tiled=True),
        preferred_element_type=jnp.float32,
    )
    d_model = head_partial.shape[1]
    residual = hidden_in.astype(jnp.float32) + lax.psum_scatter(
        head_partial.astype(jnp.bfloat16), "tp", scatter_dimension=1, tiled=True
    ).astype(jnp.float32)
    square_total = lax.psum(jnp.sum(residual * residual, -1), "tp")
    normed = (residual * lax.rsqrt(square_total[:, None] / d_model + 1e-05) * norm_gain).astype(
        jnp.bfloat16
    )
    ctx_count = lax.axis_size("ctx")
    weights = route_scores / jnp.sum(route_scores, -1, keepdims=True)
    tp_count = lax.axis_size("tp")
    top_count = routes.shape[1]
    experts = ctx_count * expert_in.shape[0]
    capacity = max(2, min(tok_rows, 3 * top_count * tok_rows // experts))
    quarter_w = d_model // tp_count
    onehot = (routes[:, :, None] == jnp.arange(experts, dtype=jnp.int32)).astype(jnp.int32)
    per_tok = jnp.sum(onehot, 1)
    position = jnp.arange(tok_rows, dtype=jnp.int32)
    earlier_rows = (position[:, None] > position[None, :]).astype(jnp.bfloat16)
    before = jnp.dot(
        earlier_rows, per_tok.astype(jnp.bfloat16), preferred_element_type=jnp.float32
    ).astype(jnp.int32)
    slot_ids = jnp.sum(onehot * before[:, None, :], -1)
    flat_index = (routes * capacity + slot_ids).reshape(-1)
    full_data = lax.all_gather(normed, "tp", axis=1, tiled=True)
    row_width = full_data.shape[1]
    spread = jnp.broadcast_to(full_data[:, None, :], (tok_rows, top_count, row_width)).reshape(
        -1, row_width
    )
    outbox = jnp.zeros((experts * capacity, row_width), jnp.bfloat16).at[flat_index].set(spread)
    arrived = lax.all_to_all(
        outbox.reshape(ctx_count, 1, capacity, row_width),
        "ctx",
        split_axis=0,
        concat_axis=1,
        tiled=True,
    )
    leading = arrived.shape[:3]
    row_data = arrived.reshape(-1, d_model)
    gate_vals = jnp.dot(row_data, expert_in[0, 0], preferred_element_type=jnp.float32)
    up_vals = jnp.dot(row_data, expert_in[0, 1], preferred_element_type=jnp.float32)
    activated = ((up_vals + 1.0) * gate_vals * jax.nn.sigmoid(1.702 * gate_vals)).astype(
        jnp.bfloat16
    )
    partial_value = jnp.dot(activated, expert_out[0], preferred_element_type=jnp.float32).astype(
        jnp.bfloat16
    )
    result = partial_value.reshape(leading + (d_model,))
    returned = lax.all_to_all(result, "ctx", split_axis=1, concat_axis=0, tiled=True)
    picked = returned.reshape(-1, d_model)[flat_index].reshape(tok_rows, top_count, d_model)
    expert_result = lax.psum_scatter(
        picked.astype(jnp.float32).astype(jnp.bfloat16), "tp", scatter_dimension=2, tiled=True
    )
    moe_sum = jnp.zeros((tok_rows, quarter_w), jnp.float32)
    for member in range(top_count):
        moe_sum = moe_sum + weights[:, member : member + 1] * expert_result[:, member].astype(
            jnp.float32
        )
    return (residual + moe_sum).astype(jnp.bfloat16)


def solution(mesh):
    in_specs = (
        P("ctx", "tp"),
        P("ctx", "tp"),
        P("ctx", "tp", None),
        P("tp"),
        P("tp", "ctx"),
        P("tp"),
        P("ctx", None, None, "tp"),
        P("ctx", "tp", None),
        P("ctx", None),
        P("ctx", None),
    )
    out_specs = P("ctx", "tp")
    return jax.shard_map(body, mesh=mesh, in_specs=in_specs, out_specs=out_specs, check_vma=False)
```

```python
import jax
import jax.numpy as jnp
from jax import lax
from jax.experimental import pallas as pl
from jax.experimental.pallas import tpu as pltpu
from jax.sharding import PartitionSpec as P

WINDOW_KEYS = 128


def shifted(value, axis, steps):
    count = lax.axis_size(axis)
    first, last = (max(0, -steps), min(count, count - steps))
    return lax.ppermute(value, axis, [(source, source + steps) for source in range(first, last)])


def attend(query_block, key_blk, value_blk, inside, sink_row_block, factor):
    score = (
        jnp.einsum("rgqd,sgd->gqrs", query_block, key_blk, preferred_element_type=jnp.float32)
        * factor
    )
    masked = jnp.where(inside, score, -1e30)
    top_score = jnp.maximum(jnp.max(masked, -1), sink_row_block[:, :, None])
    expvals = jnp.where(inside, jnp.exp(score - top_score[..., None]), 0.0)
    denominator = jnp.sum(expvals, -1) + jnp.exp(sink_row_block[:, :, None] - top_score)
    probs = (expvals / denominator[..., None]).astype(jnp.bfloat16)
    mixed = jnp.einsum("gqrs,sgd->rgqd", probs, value_blk, preferred_element_type=jnp.float32)
    return mixed.astype(jnp.bfloat16)


def expert_kernel(
    normed_ref, mine_ref, residual_ref, w_in_hbm, w_out_hbm, out_ref,
    full, part, w_in, w_out, act, from_core, from_two, from_one, from_z,
    load_sem, own_sem,
    gz_send, gz_recv, g1_send, g1_recv, g2_send, g2_recv, g3_send, g3_recv,
    rc_send, rc_recv, r2_send, r2_recv, r1_send, r1_recv, rz_send, rz_recv,
):
    ctx, x = lax.axis_index("ctx"), lax.axis_index("tp")
    z, y, c = ctx // 4, (ctx // 2) % 2, ctx % 2
    rows = normed_ref.shape[0]
    half = rows // 2
    width = normed_ref.shape[1]
    there = [z, z + 1 - 2 * (z % 2), z + 2 - 4 * (z // 2), 3 - z]

    def place(z_at, y_at, c_at):
        return z_at * 4 + y_at * 2 + c_at

    core_dev, y_dev, x_dev = (place(z, y, 1 - c), x), (place(z, 1 - y, c), x), (ctx, 1 - x)
    z_devs = [None] + [(place(there[o], y, c), x) for o in range(1, 4)]
    first_dev, second_dev = (y_dev, x_dev), (x_dev, y_dev)

    def span(z_at, y_at, c_at, chunk):
        return pl.ds(pl.multiple_of(place(z_at, y_at, c_at) * rows + chunk * half, half), half)

    def block(z_at, y_at, c_at):
        return pl.ds(pl.multiple_of(place(z_at, y_at, c_at) * rows, rows), rows)

    def remote(src, dst, send, recv, device):
        return pltpu.make_async_remote_copy(
            src_ref=src, dst_ref=dst, send_sem=send, recv_sem=recv,
            device_id=device, device_id_type=pl.DeviceIdType.MESH,
        )

    loads = [
        pltpu.make_async_copy(w_in_hbm, w_in, load_sem.at[0]),
        pltpu.make_async_copy(w_out_hbm, w_out, load_sem.at[1]),
    ]
    for load in loads:
        load.start()
    barrier = pltpu.get_barrier_semaphore()
    peers = [core_dev, y_dev, x_dev] + z_devs[1:]
    for peer in peers:
        pl.semaphore_signal(barrier, inc=1, device_id=peer, device_id_type=pl.DeviceIdType.MESH)
    pl.semaphore_wait(barrier, len(peers))

    def piece(chunk, o, one, two, core):
        y_at = y if (one if chunk == 0 else two) == 0 else 1 - y
        x_at = x if (two if chunk == 0 else one) == 0 else 1 - x
        c_at = c if core == 0 else 1 - c
        return full.at[x_at, span(there[o], y_at, c_at, chunk)]

    sends = []

    def send(src, dst, s_sem, r_sem, device):
        copy = remote(src, dst, s_sem, r_sem, device)
        copy.start()
        sends.append(copy)

    own = normed_ref
    own_copies = []
    for o in (1, 2, 3):
        for chunk in range(2):
            src = own.at[pl.ds(chunk * half, half)]
            dst = piece(chunk, 0, 0, 0, 0)
            send(src, dst, gz_send.at[chunk, o], gz_recv.at[chunk, o], z_devs[o])
    for chunk in range(2):
        keep = pltpu.make_async_copy(own.at[pl.ds(chunk * half, half)], piece(chunk, 0, 0, 0, 0), own_sem.at[chunk])
        keep.start()
        own_copies.append(keep)

    def pass_on(chunk, o, one, two):
        src = own.at[pl.ds(chunk * half, half)] if (o, one, two) == (0, 0, 0) else piece(chunk, o, one, two, 0)
        dst = piece(chunk, o, one, two, 0)
        if one == 0 and two == 0:
            send(src, dst, g1_send.at[chunk, o], g1_recv.at[chunk, o], first_dev[chunk])
        if two == 0:
            send(src, dst, g2_send.at[chunk, o, one], g2_recv.at[chunk, o, one], second_dev[chunk])
        send(src, dst, g3_send.at[chunk, o, one, two], g3_recv.at[chunk, o, one, two], core_dev)

    def arrive(dst, s_sem, r_sem):
        remote(dst, dst, s_sem, r_sem, core_dev).wait_recv()

    def line(o):
        for chunk in range(2):
            if o:
                arrive(piece(chunk, o, 0, 0, 0), gz_send.at[chunk, o], gz_recv.at[chunk, o])
            pass_on(chunk, o, 0, 0)

    def via_first(o):
        for chunk in range(2):
            arrive(piece(chunk, o, 1, 0, 0), g1_send.at[chunk, o], g1_recv.at[chunk, o])
            pass_on(chunk, o, 1, 0)

    def via_second(o):
        for one in range(2):
            for chunk in range(2):
                arrive(piece(chunk, o, one, 1, 0), g2_send.at[chunk, o, one], g2_recv.at[chunk, o, one])
                pass_on(chunk, o, one, 1)

    def gather_core(o):
        for chunk in range(2):
            for one in range(2):
                for two in range(2):
                    arrive(
                        piece(chunk, o, one, two, 1),
                        g3_send.at[chunk, o, one, two],
                        g3_recv.at[chunk, o, one, two],
                    )

    group = 4 * rows

    def compute(o):
        base = pl.multiple_of(there[o] * group, group)
        near = pl.ds(base, group)
        tile = 256

        @pl.loop(0, width // tile)
        def _(step):
            cols = pl.ds(pl.multiple_of(step * tile, tile), tile)

            def project(which):
                return jnp.dot(
                    full[0, near], w_in[which, pl.ds(0, width), cols], preferred_element_type=jnp.float32
                ) + jnp.dot(
                    full[1, near], w_in[which, pl.ds(width, width), cols], preferred_element_type=jnp.float32
                )

            gate, up = project(0), project(1)
            act[:, cols] = ((up + 1.0) * gate * jax.nn.sigmoid(1.702 * gate)).astype(jnp.bfloat16)

        for at in range(2):

            @pl.loop(0, width // tile)
            def _(step):
                start = pl.multiple_of(step * tile, tile)
                cols = pl.ds(start, tile)
                wide = pl.ds(pl.multiple_of(at * width + step * tile, tile), tile)
                value = jnp.dot(act[...], w_out[:, wide], preferred_element_type=jnp.float32)
                part[at, near, cols] = (value * mine_ref[near]).astype(jnp.bfloat16)

        for x_at in range(2):
            for y_at in range(2):
                send(
                    part.at[x_at, block(there[o], y_at, 1 - c)], from_core.at[o, x_at, y_at],
                    rc_send.at[o, x_at, y_at], rc_recv.at[o, x_at, y_at], core_dev,
                )

    def add(x_at, where, ref):
        part[x_at, where] = (
            part[x_at, where].astype(jnp.float32) + ref[...].astype(jnp.float32)
        ).astype(jnp.bfloat16)

    def reduce_core(o):
        for x_at in range(2):
            for y_at in range(2):
                got = from_core.at[o, x_at, y_at]
                arrive(got, rc_send.at[o, x_at, y_at], rc_recv.at[o, x_at, y_at])
                add(x_at, block(there[o], y_at, c), got)
        for k in range(2):
            send(
                part.at[1 - x, span(there[o], k, c, 0)], from_two.at[0, o, k],
                r2_send.at[0, o, k], r2_recv.at[0, o, k], x_dev,
            )
            send(
                part.at[k, span(there[o], 1 - y, c, 1)], from_two.at[1, o, k],
                r2_send.at[1, o, k], r2_recv.at[1, o, k], y_dev,
            )

    def reduce_two(o):
        for k in range(2):
            for chunk in range(2):
                got = from_two.at[chunk, o, k]
                arrive(got, r2_send.at[chunk, o, k], r2_recv.at[chunk, o, k])
                if chunk == 0:
                    add(x, span(there[o], k, c, 0), got)
                else:
                    add(k, span(there[o], y, c, 1), got)
        send(
            part.at[x, span(there[o], 1 - y, c, 0)], from_one.at[0, o],
            r1_send.at[0, o], r1_recv.at[0, o], y_dev,
        )
        send(
            part.at[1 - x, span(there[o], y, c, 1)], from_one.at[1, o],
            r1_send.at[1, o], r1_recv.at[1, o], x_dev,
        )

    def reduce_one(o):
        for chunk in range(2):
            got = from_one.at[chunk, o]
            arrive(got, r1_send.at[chunk, o], r1_recv.at[chunk, o])
            add(x, span(there[o], y, c, chunk), got)
            if o:
                send(
                    part.at[x, span(there[o], y, c, chunk)], from_z.at[o, chunk],
                    rz_send.at[o, chunk], rz_recv.at[o, chunk], z_devs[o],
                )

    line(0)
    via_first(0)
    line(1)
    via_second(0)
    via_first(1)
    line(2)
    via_second(1)
    via_first(2)
    line(3)
    for keep in own_copies:
        keep.wait()
    for load in loads:
        load.wait()
    gather_core(0)
    compute(0)
    via_first(3)
    via_second(2)
    gather_core(1)
    compute(1)
    reduce_core(0)
    via_second(3)
    gather_core(2)
    compute(2)
    reduce_two(0)
    reduce_core(1)
    gather_core(3)
    compute(3)
    reduce_one(0)
    reduce_core(2)
    reduce_two(1)
    reduce_core(3)
    reduce_two(2)
    reduce_one(1)
    reduce_two(3)
    reduce_one(2)
    reduce_one(3)
    for chunk in range(2):
        mine_rows = pl.ds(chunk * half, half)
        total = residual_ref[mine_rows] + part[x, span(z, y, c, chunk)].astype(jnp.float32)
        for o in range(1, 4):
            arrive(from_z.at[o, chunk], rz_send.at[o, chunk], rz_recv.at[o, chunk])
            total = total + from_z[o, chunk].astype(jnp.float32)
        out_ref[mine_rows] = total.astype(jnp.bfloat16)
    for copy in sends:
        copy.wait_send()


def front_kernel(
    q_ref, kv_ref, sink_ref, proj_ref, spread_ref, hidden_ref, gain_ref,
    residual_ref, normed_ref, table_ref,
    keys, proj, att, sums, outgoing, incoming, square_out, square_in,
    own_sem, kv_send, kv_recv, x_send, x_recv, s_send, s_recv,
    pz_send, pz_recv, py_send, py_recv, pc_send, pc_recv,
    wz_send, wz_recv, wy_send, wy_recv, wc_send, wc_recv,
):
    ctx, x = lax.axis_index("ctx"), lax.axis_index("tp")
    z, y, c = ctx // 4, (ctx // 2) % 2, ctx % 2
    there = [z, z + 1 - 2 * (z % 2), z + 2 - 4 * (z // 2), 3 - z]
    rows = q_ref.shape[0]
    wide = proj_ref.shape[0]
    count = 16

    def place(z_at, y_at, c_at):
        return z_at * 4 + y_at * 2 + c_at

    core_dev, y_dev, x_dev = (place(z, y, 1 - c), x), (place(z, 1 - y, c), x), (ctx, 1 - x)
    z_devs = [None] + [(place(there[o], y, c), x) for o in range(1, 4)]
    next_dev, last_dev = ((ctx + 1) % count, x), ((ctx + count - 1) % count, x)

    def remote(src, dst, send, recv, device):
        return pltpu.make_async_remote_copy(
            src_ref=src, dst_ref=dst, send_sem=send, recv_sem=recv,
            device_id=device, device_id_type=pl.DeviceIdType.MESH,
        )

    def columns(z_at, y_at, c_at):
        return proj.at[pl.ds(pl.multiple_of(place(z_at, y_at, c_at) * wide, 16), wide)]

    def share(z_at, y_at, c_at):
        return table_ref.at[place(z_at, y_at, c_at)]

    barrier = pltpu.get_barrier_semaphore()
    peers = [core_dev, y_dev, x_dev, next_dev, last_dev] + z_devs[1:]
    for peer in peers:
        pl.semaphore_signal(barrier, inc=1, device_id=peer, device_id_type=pl.DeviceIdType.MESH)
    pl.semaphore_wait(barrier, len(peers))

    sends = []

    def send(src, dst, s_sem, r_sem, device):
        copy = remote(src, dst, s_sem, r_sem, device)
        copy.start()
        sends.append(copy)

    def arrive(dst, s_sem, r_sem):
        remote(dst, dst, s_sem, r_sem, core_dev).wait_recv()

    send(kv_ref, keys.at[pl.ds(0, rows)], kv_send.at[0], kv_recv.at[0], next_dev)
    for o in (1, 2, 3):
        send(proj_ref, columns(z, y, c), pz_send.at[o], pz_recv.at[o], z_devs[o])
        send(spread_ref, share(z, y, c), wz_send.at[o], wz_recv.at[o], z_devs[o])
    keeps = [
        pltpu.make_async_copy(kv_ref, keys.at[pl.ds(rows, rows)], own_sem.at[0]),
        pltpu.make_async_copy(proj_ref, columns(z, y, c), own_sem.at[1]),
        pltpu.make_async_copy(spread_ref, share(z, y, c), own_sem.at[2]),
    ]
    for keep in keeps:
        keep.start()

    def pass_on(o, y_flip):
        y_at = 1 - y if y_flip else y
        own = o == 0 and not y_flip
        src = proj_ref if own else columns(there[o], y_at, c)
        small = spread_ref if own else share(there[o], y_at, c)
        if not y_flip:
            send(src, columns(there[o], y_at, c), py_send.at[o], py_recv.at[o], y_dev)
            send(small, share(there[o], y_at, c), wy_send.at[o], wy_recv.at[o], y_dev)
        send(src, columns(there[o], y_at, c), pc_send.at[o, y_flip], pc_recv.at[o, y_flip], core_dev)
        send(small, share(there[o], y_at, c), wc_send.at[o, y_flip], wc_recv.at[o, y_flip], core_dev)

    def from_line(o):
        if o:
            arrive(columns(there[o], y, c), pz_send.at[o], pz_recv.at[o])
            arrive(share(there[o], y, c), wz_send.at[o], wz_recv.at[o])
        pass_on(o, 0)

    def from_y(o):
        arrive(columns(there[o], 1 - y, c), py_send.at[o], py_recv.at[o])
        arrive(share(there[o], 1 - y, c), wy_send.at[o], wy_recv.at[o])
        pass_on(o, 1)

    def from_core(o):
        for y_flip in range(2):
            y_at = 1 - y if y_flip else y
            arrive(columns(there[o], y_at, 1 - c), pc_send.at[o, y_flip], pc_recv.at[o, y_flip])
            arrive(share(there[o], y_at, 1 - c), wc_send.at[o, y_flip], wc_recv.at[o, y_flip])

    lane = lax.broadcasted_iota(jnp.int32, (rows, 128), 1)
    query_pos = lax.broadcasted_iota(jnp.int32, (rows, 2 * rows), 0) + rows
    key_pos = lax.broadcasted_iota(jnp.int32, (rows, 2 * rows), 1)
    inside = (
        (key_pos <= query_pos)
        & (key_pos > query_pos - WINDOW_KEYS)
        & (key_pos + ctx * rows >= rows)
    )

    def attention(group):
        key_value = keys[:, group * 128 : group * 128 + 128]
        value_key = keys[:, 256 + group * 128 : 256 + group * 128 + 128]

        @pl.loop(0, 4)
        def _(step):
            pair = group * 4 + step
            cols = pl.ds(pl.multiple_of(pair * 128, 128), 128)
            both = q_ref[:, cols]
            mixed = []
            for odd in range(2):
                q = jnp.where((lane >= 64) if odd else (lane < 64), both, jnp.zeros_like(both))
                sink = sink_ref[pair * 2 + odd]
                score = lax.dot_general(
                    q, value_key if odd else key_value, (((1,), (1,)), ((), ())),
                    preferred_element_type=jnp.float32,
                ) * 0.125
                top = jnp.maximum(jnp.max(jnp.where(inside, score, -1e30), -1, keepdims=True), sink)
                vals = jnp.where(inside, jnp.exp(score - top), 0.0)
                under = jnp.sum(vals, -1, keepdims=True) + jnp.exp(sink - top)
                probs = (vals / under).astype(jnp.bfloat16)
                mixed.append(
                    jnp.dot(probs, key_value if odd else value_key, preferred_element_type=jnp.float32)
                )
            att[:, cols] = jnp.where(lane < 64, mixed[0], mixed[1]).astype(jnp.bfloat16)

    span = 4 * wide

    def project(o):
        near = pl.ds(pl.multiple_of(there[o] * span, 16), span)
        value = lax.dot_general(
            att[...], proj[near], (((1,), (1,)), ((), ())), preferred_element_type=jnp.float32
        )
        sums[there[o]] = value
        outgoing[there[o]] = value.astype(jnp.bfloat16)
        slot = there[o] % 2

        @pl.when(there[o] // 2 != x)
        def _():
            remote(
                outgoing.at[there[o]], incoming.at[slot], x_send.at[slot], x_recv.at[slot], x_dev
            ).start()

    from_line(0)
    for keep in keeps:
        keep.wait()
    arrive(keys.at[pl.ds(0, rows)], kv_send.at[0], kv_recv.at[0])
    attention(0)
    from_line(1)
    from_y(0)
    from_line(2)
    from_y(1)
    attention(1)
    from_line(3)
    from_core(0)
    project(0)
    from_y(2)
    from_core(1)
    project(1)
    from_y(3)
    from_core(2)
    project(2)
    from_core(3)
    project(3)
    squares = jnp.zeros((rows, 1), jnp.float32)
    for slot in range(2):
        arrive(incoming.at[slot], x_send.at[slot], x_recv.at[slot])
        cols = pl.ds(slot * span, span)
        value = (
            hidden_ref[:, cols].astype(jnp.float32)
            + (sums[2 * x + slot] + incoming[slot].astype(jnp.float32))
        )
        residual_ref[:, cols] = value
        squares = squares + jnp.sum(value * value, -1, keepdims=True)
    square_out[...] = jnp.broadcast_to(squares, square_out.shape)
    send(square_out, square_in, s_send.at[0], s_recv.at[0], x_dev)
    arrive(square_in, s_send.at[0], s_recv.at[0])
    total = squares + square_in[:, 0:1]
    scale = lax.rsqrt(total / (2 * residual_ref.shape[1]) + 1e-05)
    normed_ref[...] = (residual_ref[...] * scale * gain_ref[...]).astype(jnp.bfloat16)
    for slot in range(2):
        remote(
            outgoing.at[2 * (1 - x) + slot], incoming.at[slot], x_send.at[slot], x_recv.at[slot], x_dev
        ).wait_send()
    for copy in sends:
        copy.wait_send()


def dense_layer(
    hidden_in, queries, rotated_key_value, sink_logit_table, out_proj, norm_gain,
    expert_in, expert_out, routes, route_scores,
):
    rows, width = hidden_in.shape
    heads_width = queries.shape[1]
    experts = lax.axis_size("ctx")
    chosen = routes[:, :, None] == jnp.arange(experts, dtype=jnp.int32)
    spread = jnp.sum(jnp.where(chosen, route_scores[:, :, None], 0.0), 1).T
    key_value = rotated_key_value.reshape(rows, -1)
    value_key = jnp.concatenate([rotated_key_value[..., 64:], rotated_key_value[..., :64]], -1)
    pairs = jnp.concatenate([key_value, value_key.reshape(rows, -1)], 1)
    wide = out_proj.shape[1]
    dma = pltpu.SemaphoreType.DMA
    bf16, f32 = jnp.bfloat16, jnp.float32
    vmem = pl.BlockSpec(memory_space=pltpu.VMEM)
    residual, normed, table = pl.pallas_call(
        front_kernel,
        out_shape=(
            jax.ShapeDtypeStruct((rows, width), f32),
            jax.ShapeDtypeStruct((rows, width), bf16),
            jax.ShapeDtypeStruct((experts, experts, rows), f32),
        ),
        in_specs=[vmem, vmem, pl.BlockSpec(memory_space=pltpu.SMEM)] + [vmem] * 4,
        out_specs=(vmem, vmem, vmem),
        scratch_shapes=[
            pltpu.VMEM((2 * rows, 512), bf16),
            pltpu.VMEM((experts * wide, heads_width), bf16),
            pltpu.VMEM((rows, heads_width), bf16),
            pltpu.VMEM((4, rows, 4 * wide), f32),
            pltpu.VMEM((4, rows, 4 * wide), bf16),
            pltpu.VMEM((2, rows, 4 * wide), bf16),
            pltpu.VMEM((rows, 128), f32),
            pltpu.VMEM((rows, 128), f32),
            dma((3,)), dma((1,)), dma((1,)), dma((2,)), dma((2,)), dma((1,)), dma((1,)),
        ]
        + ([dma((4,))] * 4 + [dma((4, 2))] * 2) * 2,
        compiler_params=pltpu.CompilerParams(
            collective_id=2, has_side_effects=True, vmem_limit_bytes=32 * 2**20
        ),
        cost_estimate=pl.CostEstimate(flops=10**9, bytes_accessed=4 * 2**20, transcendentals=0),
    )(queries, pairs, sink_logit_table, out_proj.T, spread, hidden_in, norm_gain[None, :])
    mine = lax.dynamic_slice_in_dim(table, lax.axis_index("ctx"), 1, 1)
    mine = (mine / jnp.sum(table, 1, keepdims=True)).reshape(experts * rows, 1)
    return dense_experts(residual, normed, expert_in, expert_out, mine)


def dense_experts(residual, normed, expert_in, expert_out, mine):
    experts = lax.axis_size("ctx")
    rows, width = normed.shape
    dma = pltpu.SemaphoreType.DMA
    bf16 = jnp.bfloat16
    vmem = pl.BlockSpec(memory_space=pltpu.VMEM)
    total = experts * rows
    hidden = expert_in.shape[3]
    flops = 2 * total * hidden * width * 2 * 3
    return pl.pallas_call(
        expert_kernel,
        out_shape=jax.ShapeDtypeStruct((rows, width), bf16),
        in_specs=[vmem] * 3 + [pl.BlockSpec(memory_space=pl.ANY)] * 2,
        out_specs=vmem,
        scratch_shapes=[
            pltpu.VMEM((2, total, width), bf16),
            pltpu.VMEM((2, total, width), bf16),
            pltpu.VMEM((2, 2 * width, hidden), bf16),
            pltpu.VMEM((hidden, 2 * width), bf16),
            pltpu.VMEM((4 * rows, hidden), bf16),
            pltpu.VMEM((4, 2, 2, rows, width), bf16),
            pltpu.VMEM((2, 4, 2, rows // 2, width), bf16),
            pltpu.VMEM((2, 4, rows // 2, width), bf16),
            pltpu.VMEM((4, 2, rows // 2, width), bf16),
            dma((2,)),
            dma((2,)),
        ]
        + [dma((2, 4))] * 4
        + [dma((2, 4, 2))] * 2
        + [dma((2, 4, 2, 2))] * 2
        + [dma((4, 2, 2))] * 2
        + [dma((2, 4, 2))] * 2
        + [dma((2, 4))] * 2
        + [dma((4, 2))] * 2,
        compiler_params=pltpu.CompilerParams(
            collective_id=1, has_side_effects=True, vmem_limit_bytes=50 * 2**20
        ),
        cost_estimate=pl.CostEstimate(flops=flops, bytes_accessed=8 * 2**20, transcendentals=0),
    )(normed, mine, residual, expert_in[0], expert_out[0])


def body(
    hidden_in,
    queries,
    rotated_key_value,
    sink_logit_table,
    out_proj,
    norm_gain,
    expert_in,
    expert_out,
    routes,
    route_scores,
):
    tok_rows = hidden_in.shape[0]
    small = lax.axis_size("ctx") == 16 and lax.axis_size("tp") == 2
    if small and rotated_key_value.shape[1:] == (2, 128) and tok_rows == 128:
        return dense_layer(
            hidden_in, queries, rotated_key_value, sink_logit_table, out_proj, norm_gain,
            expert_in, expert_out, routes, route_scores,
        )
    kv_heads = rotated_key_value.shape[1]
    head_dim = rotated_key_value.shape[2] // 2
    q_heads = sink_logit_table.shape[0]
    queries_per_group = q_heads // kv_heads
    factor = head_dim ** (-0.5)
    sink_row_block = sink_logit_table.reshape(kv_heads, queries_per_group)
    earlier = shifted(rotated_key_value, "ctx", 1)
    keys_all = jnp.concatenate([earlier, rotated_key_value], 0)
    first_pos = lax.axis_index("ctx") * tok_rows
    block_row_count = min(512, tok_rows)
    query_block = queries.reshape(block_row_count, kv_heads, queries_per_group, head_dim)
    query_pos = first_pos + 0 + jnp.arange(block_row_count, dtype=jnp.int32)[:, None]
    key_pos = (
        first_pos
        + 0
        - WINDOW_KEYS
        + jnp.arange(block_row_count + WINDOW_KEYS, dtype=jnp.int32)[None, :]
    )
    inside = (key_pos <= query_pos) & (key_pos > query_pos - WINDOW_KEYS) & (key_pos >= 0)
    mixed = attend(
        query_block,
        keys_all[..., :head_dim],
        keys_all[..., head_dim:],
        inside,
        sink_row_block,
        factor,
    )
    outputs = mixed.reshape(block_row_count, q_heads * head_dim)
    head_partial = jnp.dot(
        outputs,
        lax.all_gather(out_proj, "ctx", axis=1, tiled=True),
        preferred_element_type=jnp.float32,
    )
    d_model = head_partial.shape[1]
    residual = hidden_in.astype(jnp.float32) + lax.psum_scatter(
        head_partial.astype(jnp.bfloat16), "tp", scatter_dimension=1, tiled=True
    ).astype(jnp.float32)
    square_total = lax.psum(jnp.sum(residual * residual, -1), "tp")
    normed = (residual * lax.rsqrt(square_total[:, None] / d_model + 1e-05) * norm_gain).astype(
        jnp.bfloat16
    )
    ctx_count = lax.axis_size("ctx")
    weights = route_scores / jnp.sum(route_scores, -1, keepdims=True)
    tp_count = lax.axis_size("tp")
    top_count = routes.shape[1]
    experts = ctx_count * expert_in.shape[0]
    capacity = max(2, min(tok_rows, 3 * top_count * tok_rows // experts))
    quarter_w = d_model // tp_count
    onehot = (routes[:, :, None] == jnp.arange(experts, dtype=jnp.int32)).astype(jnp.int32)
    per_tok = jnp.sum(onehot, 1)
    position = jnp.arange(tok_rows, dtype=jnp.int32)
    earlier_rows = (position[:, None] > position[None, :]).astype(jnp.bfloat16)
    before = jnp.dot(
        earlier_rows, per_tok.astype(jnp.bfloat16), preferred_element_type=jnp.float32
    ).astype(jnp.int32)
    slot_ids = jnp.sum(onehot * before[:, None, :], -1)
    flat_index = (routes * capacity + slot_ids).reshape(-1)
    full_data = lax.all_gather(normed, "tp", axis=1, tiled=True)
    row_width = full_data.shape[1]
    spread = jnp.broadcast_to(full_data[:, None, :], (tok_rows, top_count, row_width)).reshape(
        -1, row_width
    )
    outbox = jnp.zeros((experts * capacity, row_width), jnp.bfloat16).at[flat_index].set(spread)
    arrived = lax.all_to_all(
        outbox.reshape(ctx_count, 1, capacity, row_width),
        "ctx",
        split_axis=0,
        concat_axis=1,
        tiled=True,
    )
    leading = arrived.shape[:3]
    row_data = arrived.reshape(-1, d_model)
    gate_vals = jnp.dot(row_data, expert_in[0, 0], preferred_element_type=jnp.float32)
    up_vals = jnp.dot(row_data, expert_in[0, 1], preferred_element_type=jnp.float32)
    activated = ((up_vals + 1.0) * gate_vals * jax.nn.sigmoid(1.702 * gate_vals)).astype(
        jnp.bfloat16
    )
    partial_value = jnp.dot(activated, expert_out[0], preferred_element_type=jnp.float32).astype(
        jnp.bfloat16
    )
    result = partial_value.reshape(leading + (d_model,))
    returned = lax.all_to_all(result, "ctx", split_axis=1, concat_axis=0, tiled=True)
    picked = returned.reshape(-1, d_model)[flat_index].reshape(tok_rows, top_count, d_model)
    expert_result = lax.psum_scatter(
        picked.astype(jnp.float32).astype(jnp.bfloat16), "tp", scatter_dimension=2, tiled=True
    )
    moe_sum = jnp.zeros((tok_rows, quarter_w), jnp.float32)
    for member in range(top_count):
        moe_sum = moe_sum + weights[:, member : member + 1] * expert_result[:, member].astype(
            jnp.float32
        )
    return (residual + moe_sum).astype(jnp.bfloat16)


def solution(mesh):
    in_specs = (
        P("ctx", "tp"),
        P("ctx", "tp"),
        P("ctx", "tp", None),
        P("tp"),
        P("tp", "ctx"),
        P("tp"),
        P("ctx", None, None, "tp"),
        P("ctx", "tp", None),
        P("ctx", None),
        P("ctx", None),
    )
    out_specs = P("ctx", "tp")
    return jax.shard_map(body, mesh=mesh, in_specs=in_specs, out_specs=out_specs, check_vma=False)
```
